256 devices in a mesh: tm: 16 (over z, x_hi), rows: 16 (over x_lo, y, core).
Axes of the slice: x: 4 (x_hi: 2, x_lo: 2; x = x_hi * 2 + x_lo), y: 4, z: 8, core: 2. Of those that a mesh axis runs over, the one named last changes fastest.
Arguments:
- slc_stack: bfloat16 [64, 2, 128, 2048], P('tm', None, 'rows'), may hold values from -6 to 6
- partner_count: int32 [64], P('tm'), may hold values from 2 to 6, as said below
- look_sizes: int32 [64, 2], P('tm'), may hold values from 1 to 8, as said below
Outputs:
- interferogram: bfloat16 [64, 6, 2, 128, 2048], P('tm', None, None, 'rows')
- coherence: bfloat16 [64, 6, 128, 2048], P('tm', None, 'rows')
The draws below stay inside these ranges and needn't reach their ends.
Inputs may be any that keep to these rules, and one draw needn't show every extreme that they name: `partner_count`: some acquisition has 6 partners and some has 2. `look_sizes`: Half-heights run from 1 to 2, half-widths from 2 to 8; some acquisition has (2, 8) and some (1, 2).
All inputs are finite; a program needn't handle non-finite values.
Results may differ from the reference program's by a relative error of at most 0.0049.
Values may be sent and summed in bfloat16 or wider, within the bound.
No kernel may reach another device: no remote copies, remote signals or barrier semaphores. Data moves between devices by JAX's collectives and lax.ppermute only.
A program may use at most 64 MiB of HBM per device.

```python
import jax
import jax.numpy as jnp
from jax import lax

MAXP = 6
HR = 2
HC = 8
COLS = 2048
ACQ = 64
IMG_ROWS = 128


def draw_partner_count(key, part):
    key_counts = jax.random.fold_in(key, 11)
    key_top = jax.random.fold_in(key, 12)
    key_low = jax.random.fold_in(key, 13)
    counts = jax.random.randint(key_counts, (ACQ,), 2, MAXP + 1)
    top_at = jax.random.randint(key_top, (), 0, ACQ)
    low_at = (top_at + 1 + jax.random.randint(key_low, (), 0, ACQ - 1)) % ACQ
    counts = counts.at[top_at].set(MAXP).at[low_at].set(2)
    return counts.astype(jnp.int32)


def draw_look_sizes(key, part):
    key_rows = jax.random.fold_in(key, 21)
    key_cols = jax.random.fold_in(key, 22)
    key_top = jax.random.fold_in(key, 23)
    key_low = jax.random.fold_in(key, 24)
    half_rows = jax.random.randint(key_rows, (ACQ,), 1, HR + 1)
    half_cols = jax.random.randint(key_cols, (ACQ,), 2, HC + 1)
    top_at = jax.random.randint(key_top, (), 0, ACQ)
    low_at = (top_at + 1 + jax.random.randint(key_low, (), 0, ACQ - 1)) % ACQ
    half_rows = half_rows.at[top_at].set(HR).at[low_at].set(1)
    half_cols = half_cols.at[top_at].set(HC).at[low_at].set(2)
    return jnp.stack([half_rows, half_cols], 1).astype(jnp.int32)


def levels(own_key, extent, split, least, top_value):
    loudness, own = 1.0, jax.random.fold_in(own_key, 6)
    for axis_at, blocks in split:
        heights = jnp.exp(jax.random.uniform(jax.random.fold_in(own, axis_at), (blocks,), jnp.float32, least / len(split), top_value / len(split)))
        loudness = loudness * jnp.repeat(heights, extent[axis_at] // blocks).reshape([-1 if axis == axis_at else 1 for axis in range(len(extent))])
    return loudness


def normal_values(stream_key, shape, width, reach, split=(), kind=jnp.bfloat16):
    array = width * jax.random.normal(stream_key, shape, jnp.float32)
    if split:
        array = array * levels(stream_key, shape, split, -0.22, 0.18)
    return jnp.clip(array, -reach, reach).astype(kind)


def setup_inputs(seed: int = 0) -> dict:
    key_of = jax.random.split(jax.random.key(seed), 4)
    return {
        "slc_stack": normal_values(key_of[0], (ACQ, 2, IMG_ROWS, COLS), 1.0, 6.0, ((0, 16), (2, 16))),
        "partner_count": draw_partner_count(jax.random.fold_in(key_of[3], 71), 0),
        "look_sizes": draw_look_sizes(jax.random.fold_in(key_of[3], 71), 0),
    }


epsilon = 1e-06

def window_rows(fields, half_rows):
    row_count = fields.shape[-2]
    padded = jnp.pad(fields, [(0, 0)] * (fields.ndim - 2) + [(HR, HR), (0, 0)])
    total = jnp.zeros(fields.shape, jnp.float32)
    for offset in range(-HR, HR + 1):
        piece = padded[..., HR + offset:HR + offset + row_count, :]
        total = total + jnp.where(abs(offset) <= half_rows, piece, 0.0)
    return total

def window_cols(summed, half_cols):
    col_count = summed.shape[-1]
    padded = jnp.pad(summed.astype(jnp.float32), [(0, 0)] * (summed.ndim - 1) + [(HC, HC)])
    total = jnp.zeros(summed.shape, jnp.float32)
    for offset in range(-HC, HC + 1):
        piece = padded[..., HC + offset:HC + offset + col_count]
        total = total + jnp.where(abs(offset) <= half_cols, piece, 0.0)
    return total

def reference(slc_stack, partner_count, look_sizes):
    acq_total = slc_stack.shape[0]

    def one_acquisition(acq_index):
        own = lax.dynamic_index_in_dim(slc_stack, acq_index, 0, keepdims=False).astype(jnp.float32)
        half_rows = look_sizes[acq_index, 0]
        half_cols = look_sizes[acq_index, 1]
        own_power = own[0] * own[0] + own[1] * own[1]
        boxed_own = window_cols(window_rows(own_power, half_rows).astype(jnp.bfloat16), half_cols)
        offsets = jnp.arange(1, MAXP + 1, dtype=jnp.int32)
        partner_index = jnp.minimum(acq_index + offsets, acq_total - 1).astype(jnp.int32)
        partners = slc_stack[partner_index].astype(jnp.float32)
        real_part = own[0] * partners[:, 0] + own[1] * partners[:, 1]
        imag_part = own[1] * partners[:, 0] - own[0] * partners[:, 1]
        power = partners[:, 0] * partners[:, 0] + partners[:, 1] * partners[:, 1]
        terms = jnp.stack([real_part, imag_part, power], 1)
        boxed = window_cols(window_rows(terms, half_rows).astype(jnp.bfloat16), half_cols)
        live = (offsets <= partner_count[acq_index]) & (acq_index + offsets < acq_total)
        area = ((2 * half_rows + 1) * (2 * half_cols + 1)).astype(jnp.float32)
        ifg = jnp.where(live[:, None, None, None], boxed[:, :2] / area, 0.0).astype(jnp.bfloat16)
        magnitude = jnp.sqrt(boxed[:, 0] * boxed[:, 0] + boxed[:, 1] * boxed[:, 1])
        coh = magnitude * lax.rsqrt(boxed_own[None] * boxed[:, 2] + epsilon)
        coh = jnp.where(live[:, None, None], coh, 0.0).astype(jnp.bfloat16)
        return (ifg, coh)
    interferogram, coherence = lax.map(one_acquisition, jnp.arange(acq_total, dtype=jnp.int32))
    return (interferogram, coherence)
```

```python
import functools

import jax
import jax.numpy as jnp
from jax import lax
from jax.experimental import pallas as pl
from jax.experimental.pallas import tpu as pltpu
from jax.sharding import PartitionSpec as P

MAXP = 6
ROWS = 8
HALO = 2
NEAR = 10
EDGE = 2 * NEAR
FIELDS = 160
BLOCK = 256
epsilon = 1e-06
F32 = jnp.float32
BF16 = jnp.bfloat16


def iota(shape, dim):
    return lax.broadcasted_iota(jnp.int32, shape, dim)


def place():
    row = lax.axis_index("rows")
    return row, lax.rem(row, 2), lax.axis_size("rows")


def weights_kernel(looks, row_weights, bands):
    row, core, row_total = place()
    at = iota((8, 256), 1)
    halo_at = at - 152
    inside = halo_at >= 0
    inner = halo_at >= 48
    group = lax.shift_right_arithmetic(jnp.where(inner, halo_at - 48, halo_at), 4)
    near = lax.shift_right_arithmetic(halo_at, 1) & 7
    slot_ok = (near >= 1) & (near <= 6)
    halo_field = jnp.where(
        group == 2,
        jnp.where(near <= 6, 12 + near, 99),
        jnp.where(slot_ok, 6 * group + near - 1, 99),
    )
    field = jnp.where(inside, halo_field, lax.shift_right_arithmetic(at, 3))
    above = jnp.where(inner, core, 1 - core) == 1
    edge = (halo_at & 1) + jnp.where(above, -HALO, ROWS)
    position = jnp.where(inside, edge, at & 7)
    open_edge = jnp.where(core == 0, row > 0, row < row_total - 1)
    usable = ~inside | inner | open_edge
    field = jnp.where(usable & (at < 248), field, 99)
    distance = jnp.abs(position - iota((8, 256), 0))
    for a in range(4):
        hit = distance <= looks[a, 0]
        for f in range(FIELDS // 16):
            pair = [jnp.where(hit & (field == 2 * f + i), 1.0, 0.0) for i in range(2)]
            row_weights[a, 16 * f : 16 * f + 16, :] = jnp.concatenate(pair, 0).astype(BF16)
    inner_at = iota((384, 256), 0)
    column = jnp.where(
        inner_at < 320, inner_at, inner_at - 384
    )
    spread = jnp.abs(column - iota((384, 256), 1))
    for a in range(4):
        bands[a] = jnp.where(spread <= looks[a, 1], 1.0, 0.0).astype(BF16)


def edges_kernel(own, next_1, next_2, outer, inner):
    row, core, _ = place()
    to = iota((2 * 2 * EDGE, 2 * NEAR * ROWS), 0)
    source = iota((2 * 2 * EDGE, 2 * NEAR * ROWS), 1)
    is_inner = to >= 2 * EDGE
    to = jnp.where(is_inner, to - 2 * EDGE, to)
    high = jnp.where(is_inner, 1 - core, core) == 1
    wanted = lax.shift_right_arithmetic(to, 1) * ROWS + (to & 1) + jnp.where(high, ROWS - HALO, 0)
    pick = jnp.where(source == wanted, 1.0, 0.0).astype(BF16)

    def body(n, carry):
        cols = pl.ds(pl.multiple_of(n * BLOCK, BLOCK), BLOCK)
        parts = []
        for c in range(2):
            for ref in (own, next_1, next_2):
                for e in range(ref.shape[0]):
                    parts.append(ref[e, c, :, cols].astype(F32))
        data = jnp.concatenate(parts, 0).astype(BF16)
        picked = jnp.dot(pick, data, preferred_element_type=F32).astype(BF16)
        outer[:, cols] = picked[: 2 * EDGE]
        inner[:, cols] = picked[2 * EDGE :]
        return carry

    lax.fori_loop(0, own.shape[-1] // BLOCK, body, 0)


def repeated(tile, first):
    rows = iota(tile.shape, 0)
    kept = jnp.where((rows >= first) & (rows < first + 2), tile, 0.0)
    kept = kept + pltpu.roll(kept, 2, 0)
    return kept + pltpu.roll(kept, 4, 0)


def products(own_re, own_im, re, im):
    return own_re * re + own_im * im, own_im * re - own_re * im


def main_kernel(
    counts, looks, own, next_1, next_2, outer, inner, row_weights, bands,
    ifg_out, coh_out, edge_rows, sums, ifg, coh, sems,
):
    cols_total = own.shape[-1]
    blocks = cols_total // BLOCK
    sums[:, :128] = jnp.zeros((FIELDS, 128), BF16)
    sums[:, 128 + cols_total :] = jnp.zeros((FIELDS, 128), BF16)
    for h, ref in enumerate((outer, inner)):
        edge_rows[h, 2 * EDGE :, :] = jnp.zeros((8, cols_total), F32)
        edge_rows[h, : 2 * EDGE, :] = ref[...].astype(F32)
    near = [own.at[e] for e in range(4)] + [next_1.at[e] for e in range(4)] + [next_2.at[e] for e in range(2)]
    first_acq = lax.axis_index("tm") * 4
    acq_total = lax.axis_size("tm") * 4
    copies = []
    for a in range(4):
        def row_body(n, carry, a=a):
            start = pl.multiple_of(n * BLOCK, BLOCK)
            cols = pl.ds(start, BLOCK)
            res, ims, pows = [], [], []
            own_re = own[a, 0, :, cols].astype(F32)
            own_im = own[a, 1, :, cols].astype(F32)
            pows.append(own_re * own_re + own_im * own_im)
            for j in range(1, MAXP + 1):
                re = near[a + j][0, :, cols].astype(F32)
                im = near[a + j][1, :, cols].astype(F32)
                prod_re, prod_im = products(own_re, own_im, re, im)
                res.append(prod_re)
                ims.append(prod_im)
                pows.append(re * re + im * im)
            fields = res + ims + pows
            for h in range(2):
                mine = []
                for c in range(2):
                    at = c * EDGE + 2 * a
                    tile = edge_rows[h, at // 8 * 8 : at // 8 * 8 + 8, cols]
                    mine.append(repeated(tile, at % 8))
                res, ims, pows = [], [], []
                for half in range(2):
                    at = 2 * a + 8 * half
                    re = edge_rows[h, at : at + 8, cols]
                    im = edge_rows[h, at + EDGE : at + EDGE + 8, cols]
                    prod_re, prod_im = products(mine[0], mine[1], re, im)
                    res.append(prod_re)
                    ims.append(prod_im)
                    pows.append(re * re + im * im)
                fields += res + ims + pows
            fields.append(jnp.zeros((8, BLOCK), F32))
            terms = jnp.concatenate(fields, 0).astype(BF16)
            summed = jnp.dot(row_weights[a], terms, preferred_element_type=F32)
            sums[:, pl.ds(pl.multiple_of(start + 128, 128), BLOCK)] = summed.astype(BF16)
            return carry

        lax.fori_loop(0, blocks, row_body, 0)
        half_rows, half_cols = looks[a, 0], looks[a, 1]
        area = ((2 * half_rows + 1) * (2 * half_cols + 1)).astype(F32)
        lives = []
        for j in range(MAXP):
            live = (j < counts[a]) & (first_acq + a + j + 1 < acq_total)
            lives.append(jnp.where(live, 1.0, 0.0).astype(F32))

        def col_body(n, carry, a=a, lives=lives, area=area):
            start = pl.multiple_of(n * BLOCK, BLOCK)
            cols = pl.ds(start, BLOCK)
            inside = sums[:, pl.ds(pl.multiple_of(start + 128, 128), BLOCK)]
            left = sums[:, pl.ds(start, 128)]
            right = sums[:, pl.ds(pl.multiple_of(start + 128 + BLOCK, 128), 128)]
            sides = jnp.where(iota((FIELDS, 128), 1) < 64, right, left)
            boxed = jnp.dot(inside, bands[a, :BLOCK, :], preferred_element_type=F32)
            boxed = boxed + jnp.dot(sides, bands[a, BLOCK:, :], preferred_element_type=F32)
            own_power = boxed[96:104]
            for j in range(MAXP):
                re = boxed[8 * j : 8 * j + 8]
                im = boxed[48 + 8 * j : 56 + 8 * j]
                power = boxed[104 + 8 * j : 112 + 8 * j]
                scale = jnp.full((8, BLOCK), lives[j], F32) / jnp.full((8, BLOCK), area, F32)
                ifg[a, j, 0, :, cols] = (re * scale).astype(BF16)
                ifg[a, j, 1, :, cols] = (im * scale).astype(BF16)
                magnitude = jnp.sqrt(re * re + im * im)
                coherence = magnitude * lax.rsqrt(own_power * power + epsilon) * lives[j]
                coh[a, j, :, cols] = coherence.astype(BF16)
            return carry

        lax.fori_loop(0, blocks, col_body, 0)
        for k, (scratch, out) in enumerate(((ifg, ifg_out), (coh, coh_out))):
            copy = pltpu.make_async_copy(scratch.at[a], out.at[a], sems.at[a, k])
            copy.start()
            copies.append(copy)
    for copy in copies:
        copy.wait()


VMEM = pl.BlockSpec(memory_space=pltpu.VMEM)
SMEM = pl.BlockSpec(memory_space=pltpu.SMEM)
PARAMS = pltpu.CompilerParams(vmem_limit_bytes=48 * 2**20)


def shifted(block, distance):
    count = lax.axis_size("tm")
    return lax.ppermute(block, "tm", [(i, (i - distance) % count) for i in range(count)])


def local(slc_stack, partner_count, look_sizes):
    cols = slc_stack.shape[-1]
    rows = lax.axis_size("rows")
    next_1 = shifted(slc_stack, 1)
    next_2 = shifted(slc_stack[:2], 2)
    row_weights, bands = pl.pallas_call(
        weights_kernel,
        in_specs=[SMEM],
        out_specs=[VMEM, VMEM],
        out_shape=[
            jax.ShapeDtypeStruct((4, FIELDS, 256), BF16),
            jax.ShapeDtypeStruct((4, 384, 256), BF16),
        ],
        compiler_params=PARAMS,
        name="weights",
    )(look_sizes)
    edge_shape = jax.ShapeDtypeStruct((2 * EDGE, cols), BF16)
    outer, inner = pl.pallas_call(
        edges_kernel,
        in_specs=[VMEM] * 3,
        out_specs=[VMEM] * 2,
        out_shape=[edge_shape] * 2,
        compiler_params=PARAMS,
        name="edges",
    )(slc_stack, next_1, next_2)
    outer = lax.ppermute(
        outer, "rows", [((i + 1 - 2 * (1 - i % 2)) % rows, i) for i in range(rows)]
    )
    inner = lax.ppermute(inner, "rows", [(i ^ 1, i) for i in range(rows)])
    return pl.pallas_call(
        main_kernel,
        in_specs=[SMEM, SMEM] + [VMEM] * 7,
        out_specs=[pl.BlockSpec(memory_space=pl.ANY)] * 2,
        out_shape=[
            jax.ShapeDtypeStruct((4, MAXP, 2, ROWS, cols), BF16),
            jax.ShapeDtypeStruct((4, MAXP, ROWS, cols), BF16),
        ],
        scratch_shapes=[
            pltpu.VMEM((2, 2 * EDGE + 8, cols), F32),
            pltpu.VMEM((FIELDS, cols + 256), BF16),
            pltpu.VMEM((4, MAXP, 2, ROWS, cols), BF16),
            pltpu.VMEM((4, MAXP, ROWS, cols), BF16),
            pltpu.SemaphoreType.DMA((4, 2)),
        ],
        compiler_params=PARAMS,
        name="windows",
    )(partner_count, look_sizes, slc_stack, next_1, next_2, outer, inner, row_weights, bands)


def solution(mesh):
    return jax.shard_map(
        local,
        mesh=mesh,
        in_specs=(P("tm", None, "rows", None), P("tm"), P("tm", None)),
        out_specs=(P("tm", None, None, "rows", None), P("tm", None, "rows", None)),
        check_vma=False,
    )
```

```python
import jax
import jax.numpy as jnp
from jax import lax
from jax.experimental import pallas as pl
from jax.experimental.pallas import tpu as pltpu
from jax.sharding import PartitionSpec as P

MAXP = 6
ROWS = 8
HALO = 2
NEAR = 10
EDGE = 2 * NEAR
FIELDS = 160
WINDOW = 96
BLOCK = 256
PAD = 128
UNROLL_SUMS = 4
UNROLL_HALO = 4
UNROLL_COLS = 4
epsilon = 1e-06
tiny = 1.1754944e-38
F32 = jnp.float32
BF16 = jnp.bfloat16


def iota(shape, dim):
    return lax.broadcasted_iota(jnp.int32, shape, dim)


def place():
    row = lax.axis_index("rows")
    return row, lax.rem(row, 2), lax.axis_size("rows")


def setup_kernel(looks, counts, own, own_copy, main_weights, halo_weights, bands, factors):
    row, core, row_total = place()
    own_copy[...] = own[...]
    out_row = iota((8, FIELDS), 0)
    at = iota((8, FIELDS), 1)
    main_field = lax.shift_right_arithmetic(at, 3)
    main_distance = jnp.abs((at & 7) - out_row)

    halo_row = iota((8, 2 * WINDOW), 0)
    at = iota((8, 2 * WINDOW), 1)
    at = jnp.where(at >= WINDOW, at - WINDOW, at)
    inner = at >= 48
    group = lax.shift_right_arithmetic(jnp.where(inner, at - 48, at), 4)
    near = lax.shift_right_arithmetic(at, 1) & 7
    slot_ok = (near >= 1) & (near <= 6)
    power_field = jnp.where(near <= 6, 12 + near, 99)
    halo_field = jnp.where(group == 2, power_field, jnp.where(slot_ok, 6 * group + near - 1, 99))
    above = jnp.where(inner, core, 1 - core) == 1
    position = (at & 1) + jnp.where(above, -HALO, ROWS)
    open_edge = jnp.where(core == 0, row > 0, row < row_total - 1)
    halo_field = jnp.where(inner | open_edge, halo_field, 99)
    halo_distance = jnp.abs(position - halo_row)

    for a in range(4):
        for weights, distance, field in (
            (main_weights, main_distance, main_field),
            (halo_weights, halo_distance, halo_field),
        ):
            hit = distance <= looks[a, 0]
            for f in range(FIELDS // 16):
                pair = [jnp.where(hit & (field == 2 * f + i), 1.0, 0.0) for i in range(2)]
                weights[a, 16 * f : 16 * f + 16, :] = jnp.concatenate(pair, 0).astype(BF16)

    column = iota((384, BLOCK), 0)
    column = jnp.where(column < 320, column, column - 384)
    spread = jnp.abs(column - iota((384, BLOCK), 1))
    first_acq = lax.axis_index("tm") * 4
    acq_total = lax.axis_size("tm") * 4
    slot = iota((16, 128), 0)
    is_live = slot >= 8
    slot = slot & 7
    for a in range(4):
        bands[a] = jnp.where(spread <= looks[a, 1], 1.0, 0.0).astype(BF16)
        live = (slot < counts[a]) & (first_acq + a + slot + 1 < acq_total)
        area = (2 * looks[a, 0] + 1) * (2 * looks[a, 1] + 1)
        area = jnp.full((16, 128), area, jnp.int32).astype(F32)
        factors[a] = jnp.where(live, jnp.where(is_live, 1.0, 1.0 / area), 0.0)


def edges_kernel(own, next_1, next_2, outer, inner):
    row, core, _ = place()
    to = iota((2 * 2 * EDGE, 2 * NEAR * ROWS), 0)
    source = iota((2 * 2 * EDGE, 2 * NEAR * ROWS), 1)
    is_inner = to >= 2 * EDGE
    to = jnp.where(is_inner, to - 2 * EDGE, to)
    high = jnp.where(is_inner, 1 - core, core) == 1
    wanted = lax.shift_right_arithmetic(to, 1) * ROWS + (to & 1) + jnp.where(high, ROWS - HALO, 0)
    pick = jnp.where(source == wanted, 1.0, 0.0).astype(BF16)
    for n in range(own.shape[-1] // BLOCK):
        cols = slice(n * BLOCK, (n + 1) * BLOCK)
        parts = []
        for c in range(2):
            for ref in (own, next_1, next_2):
                for e in range(ref.shape[0]):
                    parts.append(ref[e, c, :, cols].astype(F32))
        data = jnp.concatenate(parts, 0).astype(BF16)
        picked = jnp.dot(pick, data, preferred_element_type=F32).astype(BF16)
        outer[:, cols] = picked[: 2 * EDGE]
        inner[:, cols] = picked[2 * EDGE :]


def halves(terms):
    high = terms.astype(BF16)
    return high, (terms - high.astype(F32)).astype(BF16)


def sums_kernel(own, next_1, next_2, main_weights, sums):
    near = [own.at[e] for e in range(4)] + [next_1.at[e] for e in range(4)]
    near += [next_2.at[e] for e in range(2)]

    def body(n, carry):
        cols = pl.ds(pl.multiple_of(n * BLOCK, BLOCK), BLOCK)
        images = [(ref[0, :, cols].astype(F32), ref[1, :, cols].astype(F32)) for ref in near]
        powers = [re * re + im * im for re, im in images]
        for a in range(4):
            own_re, own_im = images[a]
            partners = images[a + 1 : a + 1 + MAXP]
            fields = [own_re * re + own_im * im for re, im in partners]
            fields += [own_im * re - own_re * im for re, im in partners]
            fields += powers[a : a + 1 + MAXP] + [jnp.zeros((ROWS, BLOCK), F32)]
            high, low = halves(jnp.concatenate(fields, 0))
            total = jnp.dot(main_weights[a], high, preferred_element_type=F32)
            total = total + jnp.dot(main_weights[a], low, preferred_element_type=F32)
            sums[a, :, cols] = total
        return carry

    lax.fori_loop(0, sums.shape[-1] // BLOCK, body, 0, unroll=UNROLL_SUMS)


def repeated(tile, first):
    rows = iota(tile.shape, 0)
    kept = jnp.where((rows >= first) & (rows < first + 2), tile, 0.0)
    kept = kept + pltpu.roll(kept, 2, 0)
    return kept + pltpu.roll(kept, 4, 0)


def windows_kernel(
    outer, inner, halo_weights, bands, factors, sums,
    ifg_out, coh_out, edge_rows, rounded, ifg, coh, sems,
):
    cols_total = outer.shape[-1]
    blocks = cols_total // BLOCK
    rounded[:, :, :PAD] = jnp.zeros((2, FIELDS, PAD), BF16)
    rounded[:, :, PAD + cols_total :] = jnp.zeros((2, FIELDS, PAD), BF16)
    for h, ref in enumerate((outer, inner)):
        edge_rows[h, 2 * EDGE :, :] = jnp.zeros((8, cols_total), F32)
        edge_rows[h, : 2 * EDGE, :] = ref[...].astype(F32)

    def row_body(n, a):
        start = pl.multiple_of(n * BLOCK, BLOCK)
        cols = pl.ds(start, BLOCK)
        fields = []
        for h in range(2):
            mine = []
            for c in range(2):
                at = c * EDGE + 2 * a
                tile = edge_rows[h, at // 8 * 8 : at // 8 * 8 + 8, cols]
                mine.append(repeated(tile, at % 8))
            own_re, own_im = mine
            images = []
            for half in range(2):
                at = 2 * a + 8 * half
                images.append((edge_rows[h, at : at + 8, cols], edge_rows[h, at + EDGE : at + EDGE + 8, cols]))
            fields += [own_re * re + own_im * im for re, im in images]
            fields += [own_im * re - own_re * im for re, im in images]
            fields += [re * re + im * im for re, im in images]
        terms = jnp.concatenate(halves(jnp.concatenate(fields, 0)), 0)
        total = sums[a, :, cols] + jnp.dot(halo_weights[a], terms, preferred_element_type=F32)
        rounded[a % 2, :, pl.ds(pl.multiple_of(start + PAD, 128), BLOCK)] = total.astype(BF16)

    def col_body(n, a):
        start = pl.multiple_of(n * BLOCK, BLOCK)
        cols = pl.ds(start, BLOCK)
        inside = rounded[a % 2, :, pl.ds(pl.multiple_of(start + PAD, 128), BLOCK)]
        left = rounded[a % 2, :, pl.ds(start, PAD)]
        right = rounded[a % 2, :, pl.ds(pl.multiple_of(start + PAD + BLOCK, 128), PAD)]
        sides = jnp.where(iota((FIELDS, PAD), 1) < 64, right, left)
        boxed = jnp.dot(inside, bands[a, :BLOCK, :], preferred_element_type=F32)
        boxed = boxed + jnp.dot(sides, bands[a, BLOCK:, :], preferred_element_type=F32)
        own_power = boxed[96:104]
        for j in range(MAXP):
            re = boxed[8 * j : 8 * j + 8]
            im = boxed[48 + 8 * j : 56 + 8 * j]
            power = boxed[104 + 8 * j : 112 + 8 * j]
            scale = jnp.concatenate([factors[a, j : j + 1, :]] * 2, 1)
            live = jnp.concatenate([factors[a, 8 + j : 9 + j, :]] * 2, 1)
            ifg[a, j, 0, :, cols] = (re * scale).astype(BF16)
            ifg[a, j, 1, :, cols] = (im * scale).astype(BF16)
            square = re * re + im * im
            magnitude = square * lax.rsqrt(jnp.maximum(square, tiny))
            coherence = magnitude * lax.rsqrt(own_power * power + epsilon) * live
            coh[a, j, :, cols] = coherence.astype(BF16)

    def loop(body, a, unroll):
        lax.fori_loop(0, blocks, lambda n, carry: (body(n, a), carry)[1], 0, unroll=unroll)

    copies = []
    for a in range(4):
        loop(row_body, a, UNROLL_HALO)
        loop(col_body, a, UNROLL_COLS)
        for k, (scratch, out) in enumerate(((ifg, ifg_out), (coh, coh_out))):
            copy = pltpu.make_async_copy(scratch.at[a], out.at[a], sems.at[a, k])
            copy.start()
            copies.append(copy)
    for copy in copies:
        copy.wait()


VMEM = pl.BlockSpec(memory_space=pltpu.VMEM)
SMEM = pl.BlockSpec(memory_space=pltpu.SMEM)


def kernel(body, name, in_specs, out_specs, out_shape, flops, moved, scratch=(), limit=40):
    return pl.pallas_call(
        body,
        in_specs=in_specs,
        out_specs=out_specs,
        out_shape=[jax.ShapeDtypeStruct(*s) for s in out_shape],
        scratch_shapes=scratch,
        compiler_params=pltpu.CompilerParams(vmem_limit_bytes=limit * 2**20),
        cost_estimate=pl.CostEstimate(flops=flops, bytes_accessed=moved, transcendentals=0),
        name=name,
    )


def shifted(block, distance):
    count = lax.axis_size("tm")
    return lax.ppermute(block, "tm", [(i, (i - distance) % count) for i in range(count)])


def local(slc_stack, partner_count, look_sizes):
    cols = slc_stack.shape[-1]
    rows = lax.axis_size("rows")
    next_1 = shifted(slc_stack, 1)
    next_2 = shifted(slc_stack[:2], 2)
    own, main_weights, halo_weights, bands, factors = kernel(
        setup_kernel,
        "setup",
        [SMEM, SMEM, VMEM],
        [VMEM] * 5,
        [
            (slc_stack.shape, BF16),
            ((4, FIELDS, FIELDS), BF16),
            ((4, FIELDS, 2 * WINDOW), BF16),
            ((4, 384, BLOCK), BF16),
            ((4, 16, 128), F32),
        ],
        10**6,
        2 * 10**6,
    )(look_sizes, partner_count, slc_stack)
    outer, inner = kernel(
        edges_kernel, "edges", [VMEM] * 3, [VMEM] * 2, [((2 * EDGE, cols), BF16)] * 2, 10**6, 10**6
    )(own, next_1, next_2)
    outer = lax.ppermute(
        outer, "rows", [((i + 1 - 2 * (1 - i % 2)) % rows, i) for i in range(rows)]
    )
    inner = lax.ppermute(inner, "rows", [(i ^ 1, i) for i in range(rows)])
    (sums,) = kernel(
        sums_kernel,
        "sums",
        [VMEM] * 4,
        [VMEM],
        [((4, FIELDS, cols), F32)],
        4 * 10**9,
        6 * 10**6,
    )(own, next_1, next_2, main_weights)
    return kernel(
        windows_kernel,
        "windows",
        [VMEM] * 6,
        [pl.BlockSpec(memory_space=pl.ANY)] * 2,
        [((4, MAXP, 2, ROWS, cols), BF16), ((4, MAXP, ROWS, cols), BF16)],
        4 * 10**9,
        9 * 10**6,
        [
            pltpu.VMEM((2, 2 * EDGE + 8, cols), F32),
            pltpu.VMEM((2, FIELDS, cols + 2 * PAD), BF16),
            pltpu.VMEM((4, MAXP, 2, ROWS, cols), BF16),
            pltpu.VMEM((4, MAXP, ROWS, cols), BF16),
            pltpu.SemaphoreType.DMA((4, 2)),
        ],
    )(outer, inner, halo_weights, bands, factors, sums)


def solution(mesh):
    return jax.shard_map(
        local,
        mesh=mesh,
        in_specs=(P("tm", None, "rows", None), P("tm"), P("tm", None)),
        out_specs=(P("tm", None, None, "rows", None), P("tm", None, "rows", None)),
        check_vma=False,
    )
```

```python
import jax
import jax.numpy as jnp
from jax import lax
from jax.experimental import pallas as pl
from jax.experimental.pallas import tpu as pltpu
from jax.sharding import PartitionSpec as P

MAXP = 6
ROWS = 8
HALO = 2
NEAR = 10
EDGE = 24
FIELDS = 160
WINDOW = 96
BLOCK = 256
PAD = 128
UNROLL_SUMS = 8
UNROLL_HALO = 8
UNROLL_COLS = 8
epsilon = 1e-06
tiny = 1.1754944e-38
F32 = jnp.float32
BF16 = jnp.bfloat16


def iota(shape, dim):
    return lax.broadcasted_iota(jnp.int32, shape, dim)


def place():
    row = lax.axis_index("rows")
    return row, lax.rem(row, 2), lax.axis_size("rows")


def setup_kernel(looks, counts, own, own_copy, main_weights, halo_weights, bands, factors):
    row, core, row_total = place()
    own_copy[...] = own[...]
    out_row = iota((8, FIELDS), 0)
    at = iota((8, FIELDS), 1)
    main_field = lax.shift_right_arithmetic(at, 3)
    main_distance = jnp.abs((at & 7) - out_row)

    halo_row = iota((8, 2 * WINDOW), 0)
    at = iota((8, 2 * WINDOW), 1)
    at = jnp.where(at >= WINDOW, at - WINDOW, at)
    inner = at >= 48
    group = lax.shift_right_arithmetic(jnp.where(inner, at - 48, at), 4)
    near = lax.shift_right_arithmetic(at, 1) & 7
    slot_ok = (near >= 1) & (near <= 6)
    power_field = jnp.where(near <= 6, 12 + near, 99)
    halo_field = jnp.where(group == 2, power_field, jnp.where(slot_ok, 6 * group + near - 1, 99))
    above = jnp.where(inner, core, 1 - core) == 1
    position = (at & 1) + jnp.where(above, -HALO, ROWS)
    open_edge = jnp.where(core == 0, row > 0, row < row_total - 1)
    halo_field = jnp.where(inner | open_edge, halo_field, 99)
    halo_distance = jnp.abs(position - halo_row)

    for a in range(4):
        for weights, distance, field in (
            (main_weights, main_distance, main_field),
            (halo_weights, halo_distance, halo_field),
        ):
            hit = distance <= looks[a, 0]
            for f in range(FIELDS // 16):
                pair = [jnp.where(hit & (field == 2 * f + i), 1.0, 0.0) for i in range(2)]
                weights[a, 16 * f : 16 * f + 16, :] = jnp.concatenate(pair, 0).astype(BF16)

    column = iota((384, BLOCK), 0)
    column = jnp.where(column < 320, column, column - 384)
    spread = jnp.abs(column - iota((384, BLOCK), 1))
    first_acq = lax.axis_index("tm") * 4
    acq_total = lax.axis_size("tm") * 4
    slot = iota((16, 128), 0)
    is_live = slot >= 8
    slot = slot & 7
    for a in range(4):
        bands[a] = jnp.where(spread <= looks[a, 1], 1.0, 0.0).astype(BF16)
        live = (slot < counts[a]) & (first_acq + a + slot + 1 < acq_total)
        area = (2 * looks[a, 0] + 1) * (2 * looks[a, 1] + 1)
        area = jnp.full((16, 128), area, jnp.int32).astype(F32)
        factors[a] = jnp.where(live, jnp.where(is_live, 1.0, 1.0 / area), 0.0)


def picked_edges(refs, wanted, cols):
    parts = []
    for ref in refs:
        for e in range(ref.shape[0]):
            parts += [ref[e, c, :, cols].astype(F32) for c in range(2)]
    data = jnp.concatenate(parts, 0).astype(BF16)
    pick = jnp.where(iota((wanted.shape[0], data.shape[0]), 1) == wanted, 1.0, 0.0)
    return jnp.dot(pick.astype(BF16), data, preferred_element_type=F32).astype(BF16)


def own_edges_kernel(own, first_two, outer, inner, outer_two):
    core = place()[1]
    first_two[...] = own[:2]
    to = iota((40, 64), 0)
    at = to & 15
    two = jnp.where(to >= 32, 1, 0)
    image = jnp.where(two == 1, lax.shift_right_arithmetic(at, 1) & 1, lax.shift_right_arithmetic(at, 1) & 3)
    component = jnp.where(two == 1, lax.shift_right_arithmetic(at, 2), lax.shift_right_arithmetic(at, 3))
    high = jnp.where((to >= 16) & (to < 32), 1 - core, core) == 1
    wanted = (2 * image + component) * ROWS + (at & 1) + jnp.where(high, ROWS - HALO, 0)
    for n in range(own.shape[-1] // BLOCK):
        cols = slice(n * BLOCK, (n + 1) * BLOCK)
        edges = picked_edges((own,), wanted, cols)
        outer[:, cols] = edges[:16]
        inner[:, cols] = edges[16:32]
        outer_two[:, cols] = edges[32:]


def inner_edges_kernel(next_1, next_2, inner):
    core = place()[1]
    to = iota((24, 96), 0)
    at = to & 15
    two = to >= 16
    image = jnp.where(two, 4 + (lax.shift_right_arithmetic(at, 1) & 1), lax.shift_right_arithmetic(at, 1) & 3)
    component = jnp.where(two, lax.shift_right_arithmetic(at, 2), lax.shift_right_arithmetic(at, 3))
    wanted = (2 * image + component) * ROWS + (at & 1) + jnp.where(core == 0, ROWS - HALO, 0)
    for n in range(next_1.shape[-1] // BLOCK):
        cols = slice(n * BLOCK, (n + 1) * BLOCK)
        inner[:, cols] = picked_edges((next_1, next_2), wanted, cols)


def halves(terms):
    high = terms.astype(BF16)
    return high, (terms - high.astype(F32)).astype(BF16)


def sums_kernel(own, next_1, next_2, main_weights, sums):
    near = [own.at[e] for e in range(4)] + [next_1.at[e] for e in range(4)]
    near += [next_2.at[e] for e in range(2)]

    def body(n, carry):
        cols = pl.ds(pl.multiple_of(n * BLOCK, BLOCK), BLOCK)
        images = [(ref[0, :, cols].astype(F32), ref[1, :, cols].astype(F32)) for ref in near]
        powers = [re * re + im * im for re, im in images]
        for a in range(4):
            own_re, own_im = images[a]
            partners = images[a + 1 : a + 1 + MAXP]
            fields = [own_re * re + own_im * im for re, im in partners]
            fields += [own_im * re - own_re * im for re, im in partners]
            fields += powers[a : a + 1 + MAXP] + [jnp.zeros((ROWS, BLOCK), F32)]
            high, low = halves(jnp.concatenate(fields, 0))
            total = jnp.dot(main_weights[a], high, preferred_element_type=F32)
            total = total + jnp.dot(main_weights[a], low, preferred_element_type=F32)
            sums[a, :, cols] = total
        return carry

    lax.fori_loop(0, sums.shape[-1] // BLOCK, body, 0, unroll=UNROLL_SUMS)


def repeated(tile, first):
    rows = iota(tile.shape, 0)
    kept = jnp.where((rows >= first) & (rows < first + 2), tile, 0.0)
    kept = kept + pltpu.roll(kept, 2, 0)
    return kept + pltpu.roll(kept, 4, 0)


def fill_edges(edge_rows, own, next_1, next_2):
    for c in range(2):
        edge_rows[c * EDGE : c * EDGE + 8, :] = own[8 * c : 8 * c + 8]
        edge_rows[c * EDGE + 8 : c * EDGE + 16, :] = next_1[8 * c : 8 * c + 8]
        last = pltpu.roll(next_2, 4, 0) if c else next_2
        last = jnp.where(iota(last.shape, 0) < 4, last, 0.0)
        edge_rows[c * EDGE + 16 : c * EDGE + 24, :] = last


def windows_kernel(
    own_outer, outer_1, outer_2, own_inner, inner, halo_weights, bands, factors, sums,
    ifg_out, coh_out, edge_rows, rounded, ifg, coh, sems,
):
    cols_total = inner.shape[-1]
    blocks = cols_total // BLOCK
    rounded[:, :, :PAD] = jnp.zeros((2, FIELDS, PAD), BF16)
    rounded[:, :, PAD + cols_total :] = jnp.zeros((2, FIELDS, PAD), BF16)
    arrived = inner[...].astype(F32)
    fill_edges(edge_rows.at[1], own_inner[...].astype(F32), arrived[:16], arrived[16:])
    fill_edges(
        edge_rows.at[0], own_outer[...].astype(F32), outer_1[...].astype(F32), outer_2[...].astype(F32)
    )

    def row_body(n, a):
        start = pl.multiple_of(n * BLOCK, BLOCK)
        cols = pl.ds(start, BLOCK)
        fields = []
        for h in range(2):
            mine = []
            for c in range(2):
                at = c * EDGE + 2 * a
                tile = edge_rows[h, at // 8 * 8 : at // 8 * 8 + 8, cols]
                mine.append(repeated(tile, at % 8))
            own_re, own_im = mine
            images = []
            for half in range(2):
                at = 2 * a + 8 * half
                images.append((edge_rows[h, at : at + 8, cols], edge_rows[h, at + EDGE : at + EDGE + 8, cols]))
            fields += [own_re * re + own_im * im for re, im in images]
            fields += [own_im * re - own_re * im for re, im in images]
            fields += [re * re + im * im for re, im in images]
        terms = jnp.concatenate(halves(jnp.concatenate(fields, 0)), 0)
        total = sums[a, :, cols] + jnp.dot(halo_weights[a], terms, preferred_element_type=F32)
        rounded[a % 2, :, pl.ds(pl.multiple_of(start + PAD, 128), BLOCK)] = total.astype(BF16)

    def col_body(n, a):
        start = pl.multiple_of(n * BLOCK, BLOCK)
        cols = pl.ds(start, BLOCK)
        inside = rounded[a % 2, :, pl.ds(pl.multiple_of(start + PAD, 128), BLOCK)]
        left = rounded[a % 2, :, pl.ds(start, PAD)]
        right = rounded[a % 2, :, pl.ds(pl.multiple_of(start + PAD + BLOCK, 128), PAD)]
        sides = jnp.where(iota((FIELDS, PAD), 1) < 64, right, left)
        boxed = jnp.dot(inside, bands[a, :BLOCK, :], preferred_element_type=F32)
        boxed = boxed + jnp.dot(sides, bands[a, BLOCK:, :], preferred_element_type=F32)
        own_power = boxed[96:104]
        for j in range(MAXP):
            re = boxed[8 * j : 8 * j + 8]
            im = boxed[48 + 8 * j : 56 + 8 * j]
            power = boxed[104 + 8 * j : 112 + 8 * j]
            scale = jnp.concatenate([factors[a, j : j + 1, :]] * 2, 1)
            live = jnp.concatenate([factors[a, 8 + j : 9 + j, :]] * 2, 1)
            ifg[a, j, 0, :, cols] = (re * scale).astype(BF16)
            ifg[a, j, 1, :, cols] = (im * scale).astype(BF16)
            square = re * re + im * im
            magnitude = square * lax.rsqrt(jnp.maximum(square, tiny))
            coherence = magnitude * lax.rsqrt(own_power * power + epsilon) * live
            coh[a, j, :, cols] = coherence.astype(BF16)

    def loop(body, a, unroll):
        lax.fori_loop(0, blocks, lambda n, carry: (body(n, a), carry)[1], 0, unroll=unroll)

    copies = []
    for a in range(4):
        loop(row_body, a, UNROLL_HALO)
        loop(col_body, a, UNROLL_COLS)
        for k, (scratch, out) in enumerate(((ifg, ifg_out), (coh, coh_out))):
            copy = pltpu.make_async_copy(scratch.at[a], out.at[a], sems.at[a, k])
            copy.start()
            copies.append(copy)
    for copy in copies:
        copy.wait()


VMEM = pl.BlockSpec(memory_space=pltpu.VMEM)
SMEM = pl.BlockSpec(memory_space=pltpu.SMEM)


def kernel(body, name, in_specs, out_specs, out_shape, flops, moved, scratch=(), limit=40):
    return pl.pallas_call(
        body,
        in_specs=in_specs,
        out_specs=out_specs,
        out_shape=[jax.ShapeDtypeStruct(*s) for s in out_shape],
        scratch_shapes=scratch,
        compiler_params=pltpu.CompilerParams(vmem_limit_bytes=limit * 2**20),
        cost_estimate=pl.CostEstimate(flops=flops, bytes_accessed=moved, transcendentals=0),
        name=name,
    )


def moved(block, distance, partner):
    count, rows = lax.axis_size("tm"), lax.axis_size("rows")
    pairs = [
        ((t + distance) % count * rows + partner(r, rows), t * rows + r)
        for t in range(count)
        for r in range(rows)
    ]
    return lax.ppermute(block, ("tm", "rows"), pairs)


def same(row, rows):
    return row


def across(row, rows):
    return (row + 1 if row % 2 else row - 1) % rows


def sibling(row, rows):
    return row ^ 1


def local(slc_stack, partner_count, look_sizes):
    cols = slc_stack.shape[-1]
    next_1 = moved(slc_stack, 1, same)
    first_two, outer, inner, outer_two = kernel(
        own_edges_kernel,
        "own_edges",
        [VMEM],
        [VMEM] * 4,
        [((2,) + slc_stack.shape[1:], BF16), ((16, cols), BF16), ((16, cols), BF16), ((8, cols), BF16)],
        10**6,
        10**6,
    )(slc_stack)
    next_2 = moved(first_two, 2, same)
    outer_1 = moved(outer, 1, across)
    outer_2 = moved(outer_two, 2, across)
    own_outer = moved(outer, 0, across)
    own_inner = moved(inner, 0, sibling)
    own, main_weights, halo_weights, bands, factors = kernel(
        setup_kernel,
        "setup",
        [SMEM, SMEM, VMEM],
        [VMEM] * 5,
        [
            (slc_stack.shape, BF16),
            ((4, FIELDS, FIELDS), BF16),
            ((4, FIELDS, 2 * WINDOW), BF16),
            ((4, 384, BLOCK), BF16),
            ((4, 16, 128), F32),
        ],
        10**6,
        2 * 10**6,
    )(look_sizes, partner_count, slc_stack)
    (next_inner,) = kernel(
        inner_edges_kernel, "inner_edges", [VMEM] * 2, [VMEM], [((24, cols), BF16)], 10**6, 10**6
    )(next_1, next_2)
    next_inner = moved(next_inner, 0, sibling)
    (sums,) = kernel(
        sums_kernel,
        "sums",
        [VMEM] * 4,
        [VMEM],
        [((4, FIELDS, cols), F32)],
        4 * 10**9,
        6 * 10**6,
    )(own, next_1, next_2, main_weights)
    return kernel(
        windows_kernel,
        "windows",
        [VMEM] * 9,
        [pl.BlockSpec(memory_space=pl.ANY)] * 2,
        [((4, MAXP, 2, ROWS, cols), BF16), ((4, MAXP, ROWS, cols), BF16)],
        4 * 10**9,
        9 * 10**6,
        [
            pltpu.VMEM((2, 2 * EDGE, cols), F32),
            pltpu.VMEM((2, FIELDS, cols + 2 * PAD), BF16),
            pltpu.VMEM((4, MAXP, 2, ROWS, cols), BF16),
            pltpu.VMEM((4, MAXP, ROWS, cols), BF16),
            pltpu.SemaphoreType.DMA((4, 2)),
        ],
    )(own_outer, outer_1, outer_2, own_inner, next_inner, halo_weights, bands, factors, sums)


def solution(mesh):
    return jax.shard_map(
        local,
        mesh=mesh,
        in_specs=(P("tm", None, "rows", None), P("tm"), P("tm", None)),
        out_specs=(P("tm", None, None, "rows", None), P("tm", None, "rows", None)),
        check_vma=False,
    )
```

```python
import functools

import jax
import jax.numpy as jnp
from jax import lax
from jax.experimental import pallas as pl
from jax.experimental.pallas import tpu as pltpu
from jax.sharding import PartitionSpec as P

MAXP = 6
ROWS = 8
HALO = 2
NEAR = 10
EDGE = 24
FIELDS = 160
WINDOW = 96
BLOCK = 256
PAD = 128
UNROLL_SUMS = 8
UNROLL_HALO = 8
UNROLL_COLS = 8
epsilon = 1e-06
tiny = 1.1754944e-38
F32 = jnp.float32
BF16 = jnp.bfloat16


def iota(shape, dim):
    return lax.broadcasted_iota(jnp.int32, shape, dim)


def place():
    row = lax.axis_index("rows")
    return row, lax.rem(row, 2), lax.axis_size("rows")


def setup_kernel(packed, after, main_weights, halo_weights, bands, factors):
    row, core, row_total = place()
    numbers = [packed[:, a : a + 1] for a in range(4)]
    looks = [(n & 15, lax.shift_right_arithmetic(n, 4) & 15) for n in numbers]
    counts = [lax.shift_right_arithmetic(n, 8) for n in numbers]
    out_row = iota((8, FIELDS), 0)
    at = iota((8, FIELDS), 1)
    main_field = lax.shift_right_arithmetic(at, 3)
    main_distance = jnp.abs((at & 7) - out_row)

    halo_row = iota((8, 2 * WINDOW), 0)
    at = iota((8, 2 * WINDOW), 1)
    at = jnp.where(at >= WINDOW, at - WINDOW, at)
    inner = at >= 48
    group = lax.shift_right_arithmetic(jnp.where(inner, at - 48, at), 4)
    near = lax.shift_right_arithmetic(at, 1) & 7
    slot_ok = (near >= 1) & (near <= 6)
    power_field = jnp.where(near <= 6, 12 + near, 99)
    halo_field = jnp.where(group == 2, power_field, jnp.where(slot_ok, 6 * group + near - 1, 99))
    above = jnp.where(inner, core, 1 - core) == 1
    position = (at & 1) + jnp.where(above, -HALO, ROWS)
    open_edge = jnp.where(core == 0, row > 0, row < row_total - 1)
    halo_field = jnp.where(inner | open_edge, halo_field, 99)
    halo_distance = jnp.abs(position - halo_row)

    for a in range(4):
        for weights, distance, field in (
            (main_weights, main_distance, main_field),
            (halo_weights, halo_distance, halo_field),
        ):
            hit = distance <= looks[a][0]
            for f in range(FIELDS // 16):
                pair = [jnp.where(hit & (field == 2 * f + i), 1.0, 0.0) for i in range(2)]
                weights[a, 16 * f : 16 * f + 16, :] = jnp.concatenate(pair, 0).astype(BF16)

    column = iota((384, BLOCK), 0)
    column = jnp.where(column < 320, column, column - 384)
    spread = jnp.abs(column - iota((384, BLOCK), 1))
    first_acq = lax.axis_index("tm") * 4
    acq_total = lax.axis_size("tm") * 4
    slot = iota((16, 128), 0)
    is_live = slot >= 8
    slot = slot & 7
    for a in range(4):
        bands[a] = jnp.where(spread <= looks[a][1], 1.0, 0.0).astype(BF16)
        live = (slot < counts[a]) & (first_acq + a + slot + 1 < acq_total)
        area = (2 * looks[a][0] + 1) * (2 * looks[a][1] + 1)
        area = jnp.broadcast_to(area, (16, 128)).astype(F32)
        factors[a] = jnp.where(live, jnp.where(is_live, 1.0, 1.0 / area), 0.0)


def picked_edges(refs, wanted, cols):
    parts = []
    for ref in refs:
        for e in range(ref.shape[0]):
            parts += [ref[e, c, :, cols].astype(F32) for c in range(2)]
    data = jnp.concatenate(parts, 0).astype(BF16)
    pick = jnp.where(iota((wanted.shape[0], data.shape[0]), 1) == wanted, 1.0, 0.0)
    return jnp.dot(pick.astype(BF16), data, preferred_element_type=F32).astype(BF16)


def outer_rows(at, two, core):
    image = lax.shift_right_arithmetic(at, 1) & jnp.where(two, 1, 3)
    component = lax.shift_right_arithmetic(at, jnp.where(two, 2, 3))
    return (2 * image + component) * ROWS + (at & 1) + jnp.where(core == 1, ROWS - HALO, 0)


def blocks_of(ref):
    return [slice(n * BLOCK, (n + 1) * BLOCK) for n in range(ref.shape[-1] // BLOCK)]


def own_edges_kernel(images, own, first_two, outer, outer_two):
    core = place()[1]
    own[...] = images[...]
    first_two[...] = images[:2]
    to = iota((24, 64), 0)
    wanted = outer_rows(to & 15, to >= 16, core)
    for cols in blocks_of(own):
        edges = picked_edges((images,), wanted, cols)
        outer[:, cols] = edges[:16]
        outer_two[:, cols] = edges[16:]


def again_kernel(outer, outer_again):
    outer_again[...] = outer[...]


def inner_edges_kernel(*refs):
    core = place()[1]
    *images, inner = refs
    count = sum(ref.shape[0] for ref in images)
    to = iota((4 * count, 16 * count), 0)
    second = to >= 2 * count
    at = jnp.where(second, to - 2 * count, to)
    wanted = (at & -2) * ROWS + jnp.where(second, ROWS, 0) + (at & 1) + jnp.where(core == 0, ROWS - HALO, 0)
    for cols in blocks_of(inner):
        inner[:, cols] = picked_edges(images, wanted, cols)


def halves(terms):
    high = terms.astype(BF16)
    return high, (terms - high.astype(F32)).astype(BF16)


def sums_kernel(*refs):
    *blocks, main_weights, sums = refs
    near = [block.at[e] for block in blocks for e in range(block.shape[0])]
    first = len(near) - 2 - MAXP

    def body(n, carry):
        cols = pl.ds(pl.multiple_of(n * BLOCK, BLOCK), BLOCK)
        images = [(ref[0, :, cols].astype(F32), ref[1, :, cols].astype(F32)) for ref in near]
        powers = [re * re + im * im for re, im in images]
        for a in (first, first + 1):
            own_re, own_im = images[a]
            partners = images[a + 1 : a + 1 + MAXP]
            fields = [own_re * re + own_im * im for re, im in partners]
            fields += [own_im * re - own_re * im for re, im in partners]
            fields += powers[a : a + 1 + MAXP] + [jnp.zeros((ROWS, BLOCK), F32)]
            high, low = halves(jnp.concatenate(fields, 0))
            total = jnp.dot(main_weights[a], high, preferred_element_type=F32)
            total = total + jnp.dot(main_weights[a], low, preferred_element_type=F32)
            sums[a - first, :, cols] = total
        return carry

    lax.fori_loop(0, sums.shape[-1] // BLOCK, body, 0, unroll=UNROLL_SUMS)


def repeated(tile, first):
    rows = iota(tile.shape, 0)
    kept = jnp.where((rows >= first) & (rows < first + 2), tile, 0.0)
    kept = kept + pltpu.roll(kept, 2, 0)
    return kept + pltpu.roll(kept, 4, 0)


def windows_kernel(first, *refs):
    own_outer, outer_1, inner_1, *refs = refs
    outer_2, inner_2, *refs = refs if first else (None, None, *refs)
    halo_weights, bands, factors, sums, *refs = refs
    if first:
        ifg_before, coh_before, ifg_out, coh_out, *refs = refs
        edge_rows, rounded, ifg, coh, sems = refs
        pieces = [(ifg_before, ifg_out, 0), (coh_before, coh_out, 0)]
        copies = []
        for k, (ref, out, at) in enumerate(pieces):
            copies.append(pltpu.make_async_copy(ref, out.at[at : at + 2], sems.at[k]))
            copies[-1].start()
    else:
        ifg, coh, edge_rows, rounded = refs
    cols_total = inner_1.shape[-1]
    blocks = cols_total // BLOCK
    rounded[:, :, :PAD] = jnp.zeros((2, FIELDS, PAD), BF16)
    rounded[:, :, PAD + cols_total :] = jnp.zeros((2, FIELDS, PAD), BF16)
    for c in range(2):
        at = EDGE * c
        edge_rows[0, at : at + 8, :] = own_outer[8 * c : 8 * c + 8].astype(F32)
        edge_rows[0, at + 8 : at + 16, :] = outer_1[8 * c : 8 * c + 8].astype(F32)
        edge_rows[1, at : at + 16, :] = inner_1[16 * c : 16 * c + 16].astype(F32)
        for h, ref in enumerate((outer_2, inner_2)):
            last = jnp.zeros((8, cols_total), F32)
            if first:
                last = ref[...].astype(F32)
                last = pltpu.roll(last, 4, 0) if c else last
                last = jnp.where(iota(last.shape, 0) < 4, last, 0.0)
            edge_rows[h, at + 16 : at + EDGE, :] = last

    def row_body(n, a):
        start = pl.multiple_of(n * BLOCK, BLOCK)
        cols = pl.ds(start, BLOCK)
        fields = []
        for h in range(2):
            mine = []
            for c in range(2):
                at = c * EDGE + 2 * a
                tile = edge_rows[h, at // 8 * 8 : at // 8 * 8 + 8, cols]
                mine.append(repeated(tile, at % 8))
            own_re, own_im = mine
            images = []
            for half in range(2):
                at = 2 * a + 8 * half
                images.append((edge_rows[h, at : at + 8, cols], edge_rows[h, at + EDGE : at + EDGE + 8, cols]))
            fields += [own_re * re + own_im * im for re, im in images]
            fields += [own_im * re - own_re * im for re, im in images]
            fields += [re * re + im * im for re, im in images]
        terms = jnp.concatenate(halves(jnp.concatenate(fields, 0)), 0)
        total = sums[a - first, :, cols] + jnp.dot(halo_weights[a], terms, preferred_element_type=F32)
        rounded[a % 2, :, pl.ds(pl.multiple_of(start + PAD, 128), BLOCK)] = total.astype(BF16)

    def col_body(n, a):
        start = pl.multiple_of(n * BLOCK, BLOCK)
        cols = pl.ds(start, BLOCK)
        inside = rounded[a % 2, :, pl.ds(pl.multiple_of(start + PAD, 128), BLOCK)]
        left = rounded[a % 2, :, pl.ds(start, PAD)]
        right = rounded[a % 2, :, pl.ds(pl.multiple_of(start + PAD + BLOCK, 128), PAD)]
        sides = jnp.where(iota((FIELDS, PAD), 1) < 64, right, left)
        boxed = jnp.dot(inside, bands[a, :BLOCK, :], preferred_element_type=F32)
        boxed = boxed + jnp.dot(sides, bands[a, BLOCK:, :], preferred_element_type=F32)
        own_power = boxed[96:104]
        for j in range(MAXP):
            re = boxed[8 * j : 8 * j + 8]
            im = boxed[48 + 8 * j : 56 + 8 * j]
            power = boxed[104 + 8 * j : 112 + 8 * j]
            scale = jnp.concatenate([factors[a, j : j + 1, :]] * 2, 1)
            live = jnp.concatenate([factors[a, 8 + j : 9 + j, :]] * 2, 1)
            ifg[a - first, j, 0, :, cols] = (re * scale).astype(BF16)
            ifg[a - first, j, 1, :, cols] = (im * scale).astype(BF16)
            square = re * re + im * im
            magnitude = square * lax.rsqrt(jnp.maximum(square, tiny))
            coherence = magnitude * lax.rsqrt(own_power * power + epsilon) * live
            coh[a - first, j, :, cols] = coherence.astype(BF16)

    def loop(body, a, unroll):
        lax.fori_loop(0, blocks, lambda n, carry: (body(n, a), carry)[1], 0, unroll=unroll)

    for a in (first, first + 1):
        loop(row_body, a, UNROLL_HALO)
        loop(col_body, a, UNROLL_COLS)
        if first:
            for k, (scratch, out) in enumerate(((ifg, ifg_out), (coh, coh_out))):
                copy = pltpu.make_async_copy(scratch.at[a - first], out.at[a], sems.at[2 * (a - first + 1) + k])
                copy.start()
                copies.append(copy)
    if first:
        for copy in copies:
            copy.wait()


VMEM = pl.BlockSpec(memory_space=pltpu.VMEM)
SMEM = pl.BlockSpec(memory_space=pltpu.SMEM)


def kernel(body, name, in_specs, out_specs, out_shape, flops, moved, scratch=(), limit=40):
    return pl.pallas_call(
        body,
        in_specs=in_specs,
        out_specs=out_specs,
        out_shape=[jax.ShapeDtypeStruct(*s) for s in out_shape],
        scratch_shapes=scratch,
        compiler_params=pltpu.CompilerParams(vmem_limit_bytes=limit * 2**20),
        cost_estimate=pl.CostEstimate(flops=flops, bytes_accessed=moved, transcendentals=0),
        name=name,
    )


def moved(block, distance, partner):
    count, rows = lax.axis_size("tm"), lax.axis_size("rows")
    pairs = [
        ((t + distance) % count * rows + partner(r, rows), t * rows + r)
        for t in range(count)
        for r in range(rows)
    ]
    return lax.ppermute(block, ("tm", "rows"), pairs)


def same(row, rows):
    return row


def across(row, rows):
    return (row + 1 if row % 2 else row - 1) % rows


def sibling(row, rows):
    return row ^ 1


def local(slc_stack, partner_count, look_sizes):
    cols = slc_stack.shape[-1]
    edge_16, edge_8 = ((16, cols), BF16), ((8, cols), BF16)
    next_1 = moved(slc_stack, 1, same)
    own, first_two, outer, outer_two = kernel(
        own_edges_kernel,
        "own_edges",
        [VMEM],
        [VMEM] * 4,
        [(slc_stack.shape, BF16), ((2,) + slc_stack.shape[1:], BF16), edge_16, edge_8],
        10**6,
        10**6,
    )(slc_stack)
    next_2 = moved(first_two, 2, same)
    outer_2 = moved(outer_two, 2, across)
    outer_1 = moved(outer, 1, across)
    (again,) = kernel(again_kernel, "again", [VMEM], [VMEM], [edge_16], 10**5, 10**5)(outer)
    own_outer = moved(again, 0, across)
    packed = look_sizes[:, 0] + 16 * look_sizes[:, 1] + 256 * partner_count
    main_weights, halo_weights, bands, factors = kernel(
        setup_kernel,
        "setup",
        [VMEM, pl.BlockSpec(memory_space=pl.ANY)],
        [VMEM] * 4,
        [
            ((4, FIELDS, FIELDS), BF16),
            ((4, FIELDS, 2 * WINDOW), BF16),
            ((4, 384, BLOCK), BF16),
            ((4, 16, 128), F32),
        ],
        10**6,
        2 * 10**6,
    )(packed[None], again)

    anywhere = pl.BlockSpec(memory_space=pl.ANY)

    def inner_edges(name, images, after):
        count = sum(image.shape[0] for image in images)
        return kernel(
            lambda after, *refs: inner_edges_kernel(*refs),
            name,
            [anywhere] + [VMEM] * len(images),
            [VMEM],
            [((4 * count, cols), BF16)],
            10**6,
            10**6,
        )(after, *images)[0]

    def row_sums(name, blocks, after):
        return kernel(
            lambda after, *refs: sums_kernel(*refs),
            name,
            [anywhere] + [VMEM] * (len(blocks) + 1),
            [VMEM],
            [((2, FIELDS, cols), F32)],
            2 * 10**9,
            3 * 10**6,
        )(after, *blocks, main_weights)[0]

    pair_shapes = [((2, MAXP, 2, ROWS, cols), BF16), ((2, MAXP, ROWS, cols), BF16)]
    scratch = [
        pltpu.VMEM((2, 2 * EDGE, cols), F32),
        pltpu.VMEM((2, FIELDS, cols + 2 * PAD), BF16),
    ]
    edges_1 = inner_edges("inner_1", (own, next_1), factors)
    inner_1 = moved(edges_1, 0, sibling)
    sums_1 = row_sums("sums_1", (own, next_1), edges_1)
    ifg, coh = kernel(
        functools.partial(windows_kernel, 0),
        "windows_1",
        [VMEM] * 7,
        [VMEM] * 2,
        pair_shapes,
        2 * 10**9,
        4 * 10**6,
        scratch,
    )(own_outer, outer_1, inner_1, halo_weights, bands, factors, sums_1)
    edges_2 = inner_edges("inner_2", (next_2,), coh)
    inner_2 = moved(edges_2, 0, sibling)
    sums_2 = row_sums("sums_2", (own, next_1, next_2), edges_2)
    return kernel(
        functools.partial(windows_kernel, 2),
        "windows_2",
        [VMEM] * 11,
        [pl.BlockSpec(memory_space=pl.ANY)] * 2,
        [((4, MAXP, 2, ROWS, cols), BF16), ((4, MAXP, ROWS, cols), BF16)],
        2 * 10**9,
        4 * 10**6,
        scratch + [pltpu.VMEM(*shape) for shape in pair_shapes] + [pltpu.SemaphoreType.DMA((6,))],
    )(
        own_outer, outer_1, inner_1, outer_2, inner_2, halo_weights, bands, factors,
        sums_2, ifg, coh,
    )


def solution(mesh):
    return jax.shard_map(
        local,
        mesh=mesh,
        in_specs=(P("tm", None, "rows", None), P("tm"), P("tm", None)),
        out_specs=(P("tm", None, None, "rows", None), P("tm", None, "rows", None)),
        check_vma=False,
    )
```

```python
import functools

import jax
import jax.numpy as jnp
from jax import lax
from jax.experimental import pallas as pl
from jax.experimental.pallas import tpu as pltpu
from jax.sharding import PartitionSpec as P

MAXP = 6
ROWS = 8
HALO = 2
NEAR = 10
EDGE = 24
FIELDS = 160
WINDOW = 96
BLOCK = 256
PAD = 128
UNROLL_SUMS = 8
UNROLL_HALO = 8
UNROLL_COLS = 8
epsilon = 1e-06
tiny = 1.1754944e-38
F32 = jnp.float32
BF16 = jnp.bfloat16


def iota(shape, dim):
    return lax.broadcasted_iota(jnp.int32, shape, dim)


def place():
    row = lax.axis_index("rows")
    return row, lax.rem(row, 2), lax.axis_size("rows")


def setup_kernel(packed, after, main_weights, halo_weights, bands, factors):
    row, core, row_total = place()
    numbers = [packed[:, a : a + 1] for a in range(4)]
    looks = [(n & 15, lax.shift_right_arithmetic(n, 4) & 15) for n in numbers]
    counts = [lax.shift_right_arithmetic(n, 8) for n in numbers]
    out_row = iota((8, FIELDS), 0)
    at = iota((8, FIELDS), 1)
    main_field = lax.shift_right_arithmetic(at, 3)
    main_distance = jnp.abs((at & 7) - out_row)

    halo_row = iota((8, 2 * WINDOW), 0)
    at = iota((8, 2 * WINDOW), 1)
    at = jnp.where(at >= WINDOW, at - WINDOW, at)
    inner = at >= 48
    group = lax.shift_right_arithmetic(jnp.where(inner, at - 48, at), 4)
    near = lax.shift_right_arithmetic(at, 1) & 7
    slot_ok = (near >= 1) & (near <= 6)
    power_field = jnp.where(near <= 6, 12 + near, 99)
    halo_field = jnp.where(group == 2, power_field, jnp.where(slot_ok, 6 * group + near - 1, 99))
    above = jnp.where(inner, core, 1 - core) == 1
    position = (at & 1) + jnp.where(above, -HALO, ROWS)
    open_edge = jnp.where(core == 0, row > 0, row < row_total - 1)
    halo_field = jnp.where(inner | open_edge, halo_field, 99)
    halo_distance = jnp.abs(position - halo_row)

    for a in range(4):
        for weights, distance, field in (
            (main_weights, main_distance, main_field),
            (halo_weights, halo_distance, halo_field),
        ):
            hit = distance <= looks[a][0]
            for f in range(FIELDS // 16):
                pair = [jnp.where(hit & (field == 2 * f + i), 1.0, 0.0) for i in range(2)]
                weights[a, 16 * f : 16 * f + 16, :] = jnp.concatenate(pair, 0).astype(BF16)

    column = iota((384, BLOCK), 0)
    column = jnp.where(column < 320, column, column - 384)
    spread = jnp.abs(column - iota((384, BLOCK), 1))
    first_acq = lax.axis_index("tm") * 4
    acq_total = lax.axis_size("tm") * 4
    slot = iota((16, 128), 0)
    is_live = slot >= 8
    slot = slot & 7
    for a in range(4):
        bands[a] = jnp.where(spread <= looks[a][1], 1.0, 0.0).astype(BF16)
        live = (slot < counts[a]) & (first_acq + a + slot + 1 < acq_total)
        area = (2 * looks[a][0] + 1) * (2 * looks[a][1] + 1)
        area = jnp.broadcast_to(area, (16, 128)).astype(F32)
        factors[a] = jnp.where(live, jnp.where(is_live, 1.0, 1.0 / area), 0.0)


def picked_edges(refs, wanted, cols):
    parts = []
    for ref in refs:
        for e in range(ref.shape[0]):
            parts += [ref[e, c, :, cols].astype(F32) for c in range(2)]
    data = jnp.concatenate(parts, 0).astype(BF16)
    pick = jnp.where(iota((wanted.shape[0], data.shape[0]), 1) == wanted, 1.0, 0.0)
    return jnp.dot(pick.astype(BF16), data, preferred_element_type=F32).astype(BF16)


def outer_rows(at, two, core):
    image = lax.shift_right_arithmetic(at, 1) & jnp.where(two, 1, 3)
    component = lax.shift_right_arithmetic(at, jnp.where(two, 2, 3))
    return (2 * image + component) * ROWS + (at & 1) + jnp.where(core == 1, ROWS - HALO, 0)


def blocks_of(ref):
    return [slice(n * BLOCK, (n + 1) * BLOCK) for n in range(ref.shape[-1] // BLOCK)]


def own_edges_kernel(images, own, first_two, outer, outer_two):
    core = place()[1]
    own[...] = images[...]
    first_two[...] = images[:2]
    to = iota((24, 64), 0)
    wanted = outer_rows(to & 15, to >= 16, core)
    for cols in blocks_of(own):
        edges = picked_edges((images,), wanted, cols)
        outer[:, cols] = edges[:16]
        outer_two[:, cols] = edges[16:]


def again_kernel(outer, outer_again):
    outer_again[...] = outer[...]


def inner_edges_kernel(*refs):
    core = place()[1]
    *images, inner = refs
    count = sum(ref.shape[0] for ref in images)
    to = iota((4 * count, 16 * count), 0)
    second = to >= 2 * count
    at = jnp.where(second, to - 2 * count, to)
    wanted = (at & -2) * ROWS + jnp.where(second, ROWS, 0) + (at & 1) + jnp.where(core == 0, ROWS - HALO, 0)
    for cols in blocks_of(inner):
        inner[:, cols] = picked_edges(images, wanted, cols)


def halves(terms):
    high = terms.astype(BF16)
    return high, (terms - high.astype(F32)).astype(BF16)


def sums_kernel(*refs):
    *blocks, main_weights, sums = refs
    near = [block.at[e] for block in blocks for e in range(block.shape[0])]
    first = len(near) - 2 - MAXP

    def body(n, carry):
        cols = pl.ds(pl.multiple_of(n * BLOCK, BLOCK), BLOCK)
        images = [(ref[0, :, cols].astype(F32), ref[1, :, cols].astype(F32)) for ref in near]
        powers = [re * re + im * im for re, im in images]
        for a in (first, first + 1):
            own_re, own_im = images[a]
            partners = images[a + 1 : a + 1 + MAXP]
            fields = [own_re * re + own_im * im for re, im in partners]
            fields += [own_im * re - own_re * im for re, im in partners]
            fields += powers[a : a + 1 + MAXP] + [jnp.zeros((ROWS, BLOCK), F32)]
            high, low = halves(jnp.concatenate(fields, 0))
            total = jnp.dot(main_weights[a], high, preferred_element_type=F32)
            total = total + jnp.dot(main_weights[a], low, preferred_element_type=F32)
            sums[a - first, :, cols] = total
        return carry

    lax.fori_loop(0, sums.shape[-1] // BLOCK, body, 0, unroll=UNROLL_SUMS)


def repeated(tile, first):
    rows = iota(tile.shape, 0)
    kept = jnp.where((rows >= first) & (rows < first + 2), tile, 0.0)
    kept = kept + pltpu.roll(kept, 2, 0)
    return kept + pltpu.roll(kept, 4, 0)


def windows_kernel(first, *refs):
    own_outer, outer_1, inner_1, *refs = refs
    outer_2, inner_2, *refs = refs if first else (None, None, *refs)
    halo_weights, bands, factors, sums, *refs = refs
    if first:
        ifg_before, coh_before, ifg_out, coh_out, *refs = refs
        edge_rows, rounded, ifg, coh, sems = refs
        pieces = [(ifg_before, ifg_out, 0), (coh_before, coh_out, 0)]
        copies = []
        for k, (ref, out, at) in enumerate(pieces):
            copies.append(pltpu.make_async_copy(ref, out.at[at : at + 2], sems.at[k]))
            copies[-1].start()
    else:
        ifg, coh, edge_rows, rounded = refs
    cols_total = inner_1.shape[-1]
    blocks = cols_total // BLOCK
    rounded[:, :, :PAD] = jnp.zeros((2, FIELDS, PAD), BF16)
    rounded[:, :, PAD + cols_total :] = jnp.zeros((2, FIELDS, PAD), BF16)
    for c in range(2):
        at = EDGE * c
        edge_rows[0, at : at + 8, :] = own_outer[8 * c : 8 * c + 8].astype(F32)
        edge_rows[0, at + 8 : at + 16, :] = outer_1[8 * c : 8 * c + 8].astype(F32)
        edge_rows[1, at : at + 16, :] = inner_1[16 * c : 16 * c + 16].astype(F32)
        for h, ref in enumerate((outer_2, inner_2)):
            last = jnp.zeros((8, cols_total), F32)
            if first:
                last = ref[...].astype(F32)
                last = pltpu.roll(last, 4, 0) if c else last
                last = jnp.where(iota(last.shape, 0) < 4, last, 0.0)
            edge_rows[h, at + 16 : at + EDGE, :] = last

    def row_body(n, a):
        start = pl.multiple_of(n * BLOCK, BLOCK)
        cols = pl.ds(start, BLOCK)
        fields = []
        for h in range(2):
            mine = []
            for c in range(2):
                at = c * EDGE + 2 * a
                tile = edge_rows[h, at // 8 * 8 : at // 8 * 8 + 8, cols]
                mine.append(repeated(tile, at % 8))
            own_re, own_im = mine
            images = []
            for half in range(2):
                at = 2 * a + 8 * half
                images.append((edge_rows[h, at : at + 8, cols], edge_rows[h, at + EDGE : at + EDGE + 8, cols]))
            fields += [own_re * re + own_im * im for re, im in images]
            fields += [own_im * re - own_re * im for re, im in images]
            fields += [re * re + im * im for re, im in images]
        terms = jnp.concatenate(halves(jnp.concatenate(fields, 0)), 0)
        total = sums[a - first, :, cols] + jnp.dot(halo_weights[a], terms, preferred_element_type=F32)
        rounded[a % 2, :, pl.ds(pl.multiple_of(start + PAD, 128), BLOCK)] = total.astype(BF16)

    def col_body(n, a):
        start = pl.multiple_of(n * BLOCK, BLOCK)
        cols = pl.ds(start, BLOCK)
        inside = rounded[a % 2, :, pl.ds(pl.multiple_of(start + PAD, 128), BLOCK)]
        left = rounded[a % 2, :, pl.ds(start, PAD)]
        right = rounded[a % 2, :, pl.ds(pl.multiple_of(start + PAD + BLOCK, 128), PAD)]
        sides = jnp.where(iota((FIELDS, PAD), 1) < 64, right, left)
        boxed = jnp.dot(inside, bands[a, :BLOCK, :], preferred_element_type=F32)
        boxed = boxed + jnp.dot(sides, bands[a, BLOCK:, :], preferred_element_type=F32)
        own_power = boxed[96:104]
        for j in range(MAXP):
            re = boxed[8 * j : 8 * j + 8]
            im = boxed[48 + 8 * j : 56 + 8 * j]
            power = boxed[104 + 8 * j : 112 + 8 * j]
            scale = jnp.concatenate([factors[a, j : j + 1, :]] * 2, 1)
            live = jnp.concatenate([factors[a, 8 + j : 9 + j, :]] * 2, 1)
            ifg[a - first, j, 0, :, cols] = (re * scale).astype(BF16)
            ifg[a - first, j, 1, :, cols] = (im * scale).astype(BF16)
            square = re * re + im * im
            magnitude = square * lax.rsqrt(jnp.maximum(square, tiny))
            coherence = magnitude * lax.rsqrt(own_power * power + epsilon) * live
            coh[a - first, j, :, cols] = coherence.astype(BF16)

    def loop(body, a, unroll):
        lax.fori_loop(0, blocks, lambda n, carry: (body(n, a), carry)[1], 0, unroll=unroll)

    for a in (first, first + 1):
        loop(row_body, a, UNROLL_HALO)
        loop(col_body, a, UNROLL_COLS)
        if first:
            for k, (scratch, out) in enumerate(((ifg, ifg_out), (coh, coh_out))):
                copy = pltpu.make_async_copy(scratch.at[a - first], out.at[a], sems.at[2 * (a - first + 1) + k])
                copy.start()
                copies.append(copy)
    if first:
        for copy in copies:
            copy.wait()


VMEM = pl.BlockSpec(memory_space=pltpu.VMEM)
SMEM = pl.BlockSpec(memory_space=pltpu.SMEM)


def kernel(body, name, in_specs, out_specs, out_shape, flops, moved, scratch=(), limit=40):
    return pl.pallas_call(
        body,
        in_specs=in_specs,
        out_specs=out_specs,
        out_shape=[jax.ShapeDtypeStruct(*s) for s in out_shape],
        scratch_shapes=scratch,
        compiler_params=pltpu.CompilerParams(vmem_limit_bytes=limit * 2**20),
        cost_estimate=pl.CostEstimate(flops=flops, bytes_accessed=moved, transcendentals=0),
        name=name,
    )


def moved(block, distance, partner):
    count, rows = lax.axis_size("tm"), lax.axis_size("rows")
    pairs = []
    for t in range(count):
        for r in range(rows):
            source = partner(r, rows)
            if t + distance >= count:
                source = (r + rows // 2) % rows if distance == 1 else r
            elif distance and abs(source - r) > 1:
                source = r
            pairs.append(((t + distance) % count * rows + source, t * rows + r))
    return lax.ppermute(block, ("tm", "rows"), pairs)


def same(row, rows):
    return row


def across(row, rows):
    return (row + 1 if row % 2 else row - 1) % rows


def sibling(row, rows):
    return row ^ 1


def local(slc_stack, partner_count, look_sizes):
    cols = slc_stack.shape[-1]
    edge_16, edge_8 = ((16, cols), BF16), ((8, cols), BF16)
    next_1 = moved(slc_stack, 1, same)
    own, first_two, outer, outer_two = kernel(
        own_edges_kernel,
        "own_edges",
        [VMEM],
        [VMEM] * 4,
        [(slc_stack.shape, BF16), ((2,) + slc_stack.shape[1:], BF16), edge_16, edge_8],
        10**6,
        10**6,
    )(slc_stack)
    next_2 = moved(first_two, 2, same)
    outer_2 = moved(outer_two, 2, across)
    outer_1 = moved(outer, 1, across)
    (again,) = kernel(again_kernel, "again", [VMEM], [VMEM], [edge_16], 10**5, 10**5)(outer)
    own_outer = moved(again, 0, across)
    packed = look_sizes[:, 0] + 16 * look_sizes[:, 1] + 256 * partner_count
    main_weights, halo_weights, bands, factors = kernel(
        setup_kernel,
        "setup",
        [VMEM, pl.BlockSpec(memory_space=pl.ANY)],
        [VMEM] * 4,
        [
            ((4, FIELDS, FIELDS), BF16),
            ((4, FIELDS, 2 * WINDOW), BF16),
            ((4, 384, BLOCK), BF16),
            ((4, 16, 128), F32),
        ],
        10**6,
        2 * 10**6,
    )(packed[None], again)

    anywhere = pl.BlockSpec(memory_space=pl.ANY)

    def inner_edges(name, images, after):
        count = sum(image.shape[0] for image in images)
        return kernel(
            lambda after, *refs: inner_edges_kernel(*refs),
            name,
            [anywhere] + [VMEM] * len(images),
            [VMEM],
            [((4 * count, cols), BF16)],
            10**6,
            10**6,
        )(after, *images)[0]

    def row_sums(name, blocks, after):
        return kernel(
            lambda after, *refs: sums_kernel(*refs),
            name,
            [anywhere] + [VMEM] * (len(blocks) + 1),
            [VMEM],
            [((2, FIELDS, cols), F32)],
            2 * 10**9,
            3 * 10**6,
        )(after, *blocks, main_weights)[0]

    pair_shapes = [((2, MAXP, 2, ROWS, cols), BF16), ((2, MAXP, ROWS, cols), BF16)]
    scratch = [
        pltpu.VMEM((2, 2 * EDGE, cols), F32),
        pltpu.VMEM((2, FIELDS, cols + 2 * PAD), BF16),
    ]
    edges_1 = inner_edges("inner_1", (own, next_1), factors)
    inner_1 = moved(edges_1, 0, sibling)
    sums_1 = row_sums("sums_1", (own, next_1), edges_1)
    ifg, coh = kernel(
        functools.partial(windows_kernel, 0),
        "windows_1",
        [VMEM] * 7,
        [VMEM] * 2,
        pair_shapes,
        2 * 10**9,
        4 * 10**6,
        scratch,
    )(own_outer, outer_1, inner_1, halo_weights, bands, factors, sums_1)
    edges_2 = inner_edges("inner_2", (next_2,), coh)
    inner_2 = moved(edges_2, 0, sibling)
    sums_2 = row_sums("sums_2", (own, next_1, next_2), edges_2)
    return kernel(
        functools.partial(windows_kernel, 2),
        "windows_2",
        [VMEM] * 11,
        [pl.BlockSpec(memory_space=pl.ANY)] * 2,
        [((4, MAXP, 2, ROWS, cols), BF16), ((4, MAXP, ROWS, cols), BF16)],
        2 * 10**9,
        4 * 10**6,
        scratch + [pltpu.VMEM(*shape) for shape in pair_shapes] + [pltpu.SemaphoreType.DMA((6,))],
    )(
        own_outer, outer_1, inner_1, outer_2, inner_2, halo_weights, bands, factors,
        sums_2, ifg, coh,
    )


def solution(mesh):
    return jax.shard_map(
        local,
        mesh=mesh,
        in_specs=(P("tm", None, "rows", None), P("tm"), P("tm", None)),
        out_specs=(P("tm", None, None, "rows", None), P("tm", None, "rows", None)),
        check_vma=False,
    )
```

```python
import functools

import jax
import jax.numpy as jnp
from jax import lax
from jax.experimental import pallas as pl
from jax.experimental.pallas import tpu as pltpu
from jax.sharding import PartitionSpec as P

MAXP = 6
ROWS = 8
HALO = 2
NEAR = 10
EDGE = 24
FIELDS = 160
WINDOW = 96
BLOCK = 256
PAD = 128
UNROLL_SUMS = 8
UNROLL_HALO = 8
UNROLL_COLS = 8
epsilon = 1e-06
tiny = 1.1754944e-38
F32 = jnp.float32
BF16 = jnp.bfloat16


def iota(shape, dim):
    return lax.broadcasted_iota(jnp.int32, shape, dim)


def place():
    row = lax.axis_index("rows")
    return row, lax.rem(row, 2), lax.axis_size("rows")


def setup_kernel(packed, after, main_weights, halo_weights, bands, factors):
    row, core, row_total = place()
    numbers = [packed[:, a : a + 1] for a in range(4)]
    looks = [(n & 15, lax.shift_right_arithmetic(n, 4) & 15) for n in numbers]
    counts = [lax.shift_right_arithmetic(n, 8) for n in numbers]
    out_row = iota((8, FIELDS), 0)
    at = iota((8, FIELDS), 1)
    main_field = lax.shift_right_arithmetic(at, 3)
    main_distance = jnp.abs((at & 7) - out_row)

    halo_row = iota((8, 2 * WINDOW), 0)
    at = iota((8, 2 * WINDOW), 1)
    at = jnp.where(at >= WINDOW, at - WINDOW, at)
    inner = at >= 48
    group = lax.shift_right_arithmetic(jnp.where(inner, at - 48, at), 4)
    near = lax.shift_right_arithmetic(at, 1) & 7
    slot_ok = (near >= 1) & (near <= 6)
    power_field = jnp.where(near <= 6, 12 + near, 99)
    halo_field = jnp.where(group == 2, power_field, jnp.where(slot_ok, 6 * group + near - 1, 99))
    above = jnp.where(inner, core, 1 - core) == 1
    position = (at & 1) + jnp.where(above, -HALO, ROWS)
    open_edge = jnp.where(core == 0, row > 0, row < row_total - 1)
    halo_field = jnp.where(inner | open_edge, halo_field, 99)
    halo_distance = jnp.abs(position - halo_row)

    for a in range(4):
        for weights, distance, field in (
            (main_weights, main_distance, main_field),
            (halo_weights, halo_distance, halo_field),
        ):
            hit = distance <= looks[a][0]
            for f in range(FIELDS // 16):
                pair = [jnp.where(hit & (field == 2 * f + i), 1.0, 0.0) for i in range(2)]
                weights[a, 16 * f : 16 * f + 16, :] = jnp.concatenate(pair, 0).astype(BF16)

    column = iota((384, BLOCK), 0)
    column = jnp.where(column < 320, column, column - 384)
    spread = jnp.abs(column - iota((384, BLOCK), 1))
    first_acq = lax.axis_index("tm") * 4
    acq_total = lax.axis_size("tm") * 4
    slot = iota((16, 128), 0)
    is_live = slot >= 8
    slot = slot & 7
    for a in range(4):
        bands[a] = jnp.where(spread <= looks[a][1], 1.0, 0.0).astype(BF16)
        live = (slot < counts[a]) & (first_acq + a + slot + 1 < acq_total)
        area = (2 * looks[a][0] + 1) * (2 * looks[a][1] + 1)
        area = jnp.broadcast_to(area, (16, 128)).astype(F32)
        factors[a] = jnp.where(live, jnp.where(is_live, 1.0, 1.0 / area), 0.0)


def picked_edges(refs, wanted, cols):
    parts = []
    for ref in refs:
        for e in range(ref.shape[0]):
            parts += [ref[e, c, :, cols].astype(F32) for c in range(2)]
    data = jnp.concatenate(parts, 0).astype(BF16)
    pick = jnp.where(iota((wanted.shape[0], data.shape[0]), 1) == wanted, 1.0, 0.0)
    return jnp.dot(pick.astype(BF16), data, preferred_element_type=F32).astype(BF16)


def outer_rows(at, two, core):
    image = lax.shift_right_arithmetic(at, 1) & jnp.where(two, 1, 3)
    component = lax.shift_right_arithmetic(at, jnp.where(two, 2, 3))
    return (2 * image + component) * ROWS + (at & 1) + jnp.where(core == 1, ROWS - HALO, 0)


def blocks_of(ref):
    return [slice(n * BLOCK, (n + 1) * BLOCK) for n in range(ref.shape[-1] // BLOCK)]


def own_edges_kernel(images, own, first_two, outer, outer_two):
    core = place()[1]
    own[...] = images[...]
    first_two[...] = images[:2]
    to = iota((24, 64), 0)
    wanted = outer_rows(to & 15, to >= 16, core)
    for cols in blocks_of(own):
        edges = picked_edges((images,), wanted, cols)
        outer[:, cols] = edges[:16]
        outer_two[:, cols] = edges[16:]


def again_kernel(outer, outer_again):
    outer_again[...] = outer[...]


def inner_edges_kernel(*refs):
    core = place()[1]
    *images, inner = refs
    count = sum(ref.shape[0] for ref in images)
    to = iota((4 * count, 16 * count), 0)
    second = to >= 2 * count
    at = jnp.where(second, to - 2 * count, to)
    wanted = (at & -2) * ROWS + jnp.where(second, ROWS, 0) + (at & 1) + jnp.where(core == 0, ROWS - HALO, 0)
    for cols in blocks_of(inner):
        inner[:, cols] = picked_edges(images, wanted, cols)


def halves(terms):
    high = terms.astype(BF16)
    return high, (terms - high.astype(F32)).astype(BF16)


def sums_kernel(*refs):
    *blocks, main_weights, sums = refs
    near = [block.at[e] for block in blocks for e in range(block.shape[0])]
    first = len(near) - 2 - MAXP

    def body(n, carry):
        cols = pl.ds(pl.multiple_of(n * BLOCK, BLOCK), BLOCK)
        images = [(ref[0, :, cols].astype(F32), ref[1, :, cols].astype(F32)) for ref in near]
        powers = [re * re + im * im for re, im in images]
        for a in (first, first + 1):
            own_re, own_im = images[a]
            partners = images[a + 1 : a + 1 + MAXP]
            fields = [own_re * re + own_im * im for re, im in partners]
            fields += [own_im * re - own_re * im for re, im in partners]
            fields += powers[a : a + 1 + MAXP] + [jnp.zeros((ROWS, BLOCK), F32)]
            high, low = halves(jnp.concatenate(fields, 0))
            total = jnp.dot(main_weights[a], high, preferred_element_type=F32)
            total = total + jnp.dot(main_weights[a], low, preferred_element_type=F32)
            sums[a - first, :, cols] = total
        return carry

    lax.fori_loop(0, sums.shape[-1] // BLOCK, body, 0, unroll=UNROLL_SUMS)


def repeated(tile, first):
    rows = iota(tile.shape, 0)
    kept = jnp.where((rows >= first) & (rows < first + 2), tile, 0.0)
    kept = kept + pltpu.roll(kept, 2, 0)
    return kept + pltpu.roll(kept, 4, 0)


def windows_kernel(first, *refs):
    own_outer, outer_1, inner_1, *refs = refs
    outer_2, inner_2, *refs = refs if first else (None, None, *refs)
    halo_weights, bands, factors, sums, *refs = refs
    if first:
        ifg_before, coh_before, ifg_out, coh_out, *refs = refs
        edge_rows, rounded, ifg, coh, sems = refs
        pieces = [(ifg_before, ifg_out, 0), (coh_before, coh_out, 0)]
        copies = []
        for k, (ref, out, at) in enumerate(pieces):
            copies.append(pltpu.make_async_copy(ref, out.at[at : at + 2], sems.at[k]))
            copies[-1].start()
    else:
        ifg, coh, edge_rows, rounded = refs
    cols_total = inner_1.shape[-1]
    blocks = cols_total // BLOCK
    rounded[:, :, :PAD] = jnp.zeros((2, FIELDS, PAD), BF16)
    rounded[:, :, PAD + cols_total :] = jnp.zeros((2, FIELDS, PAD), BF16)
    for c in range(2):
        at = EDGE * c
        edge_rows[0, at : at + 8, :] = own_outer[8 * c : 8 * c + 8].astype(F32)
        edge_rows[0, at + 8 : at + 16, :] = outer_1[8 * c : 8 * c + 8].astype(F32)
        edge_rows[1, at : at + 16, :] = inner_1[16 * c : 16 * c + 16].astype(F32)
        for h, ref in enumerate((outer_2, inner_2)):
            last = jnp.zeros((8, cols_total), F32)
            if first:
                last = ref[...].astype(F32)
                last = pltpu.roll(last, 4, 0) if c else last
                last = jnp.where(iota(last.shape, 0) < 4, last, 0.0)
            edge_rows[h, at + 16 : at + EDGE, :] = last

    def row_body(n, a):
        start = pl.multiple_of(n * BLOCK, BLOCK)
        cols = pl.ds(start, BLOCK)
        fields = []
        for h in range(2):
            mine = []
            for c in range(2):
                at = c * EDGE + 2 * a
                tile = edge_rows[h, at // 8 * 8 : at // 8 * 8 + 8, cols]
                mine.append(repeated(tile, at % 8))
            own_re, own_im = mine
            images = []
            for half in range(2):
                at = 2 * a + 8 * half
                images.append((edge_rows[h, at : at + 8, cols], edge_rows[h, at + EDGE : at + EDGE + 8, cols]))
            fields += [own_re * re + own_im * im for re, im in images]
            fields += [own_im * re - own_re * im for re, im in images]
            fields += [re * re + im * im for re, im in images]
        terms = jnp.concatenate(halves(jnp.concatenate(fields, 0)), 0)
        total = sums[a - first, :, cols] + jnp.dot(halo_weights[a], terms, preferred_element_type=F32)
        rounded[a % 2, :, pl.ds(pl.multiple_of(start + PAD, 128), BLOCK)] = total.astype(BF16)

    def col_body(n, a):
        start = pl.multiple_of(n * BLOCK, BLOCK)
        cols = pl.ds(start, BLOCK)
        inside = rounded[a % 2, :, pl.ds(pl.multiple_of(start + PAD, 128), BLOCK)]
        left = rounded[a % 2, :, pl.ds(start, PAD)]
        right = rounded[a % 2, :, pl.ds(pl.multiple_of(start + PAD + BLOCK, 128), PAD)]
        sides = jnp.where(iota((FIELDS, PAD), 1) < 64, right, left)
        boxed = jnp.dot(inside, bands[a, :BLOCK, :], preferred_element_type=F32)
        boxed = boxed + jnp.dot(sides, bands[a, BLOCK:, :], preferred_element_type=F32)
        own_power = boxed[96:104]
        for j in range(MAXP):
            re = boxed[8 * j : 8 * j + 8]
            im = boxed[48 + 8 * j : 56 + 8 * j]
            power = boxed[104 + 8 * j : 112 + 8 * j]
            scale = jnp.concatenate([factors[a, j : j + 1, :]] * 2, 1)
            live = jnp.concatenate([factors[a, 8 + j : 9 + j, :]] * 2, 1)
            ifg[a - first, j, 0, :, cols] = (re * scale).astype(BF16)
            ifg[a - first, j, 1, :, cols] = (im * scale).astype(BF16)
            square = re * re + im * im
            magnitude = square * lax.rsqrt(jnp.maximum(square, tiny))
            coherence = magnitude * lax.rsqrt(own_power * power + epsilon) * live
            coh[a - first, j, :, cols] = coherence.astype(BF16)

    def loop(body, a, unroll):
        lax.fori_loop(0, blocks, lambda n, carry: (body(n, a), carry)[1], 0, unroll=unroll)

    for a in (first, first + 1):
        loop(row_body, a, UNROLL_HALO)
        loop(col_body, a, UNROLL_COLS)
        if first:
            for k, (scratch, out) in enumerate(((ifg, ifg_out), (coh, coh_out))):
                copy = pltpu.make_async_copy(scratch.at[a - first], out.at[a], sems.at[2 * (a - first + 1) + k])
                copy.start()
                copies.append(copy)
    if first:
        for copy in copies:
            copy.wait()


VMEM = pl.BlockSpec(memory_space=pltpu.VMEM)
SMEM = pl.BlockSpec(memory_space=pltpu.SMEM)


def kernel(body, name, in_specs, out_specs, out_shape, flops, moved, scratch=(), limit=40):
    return pl.pallas_call(
        body,
        in_specs=in_specs,
        out_specs=out_specs,
        out_shape=[jax.ShapeDtypeStruct(*s) for s in out_shape],
        scratch_shapes=scratch,
        compiler_params=pltpu.CompilerParams(vmem_limit_bytes=limit * 2**20),
        cost_estimate=pl.CostEstimate(flops=flops, bytes_accessed=moved, transcendentals=0),
        name=name,
    )


def moved(block, distance, partner):
    count, rows = lax.axis_size("tm"), lax.axis_size("rows")
    half = rows // 2
    pairs = []
    for t in range(count):
        for r in range(rows):
            start, source = (t + distance) % count, partner(r, rows)
            if t + distance >= count:
                late = {half - 1: rows - 1, half: rows - 2, rows - 1: half - 1, rows - 2: half}
                source = (r + half) % rows if distance == 1 else r
                if distance == 2 and partner is same:
                    source = late.get(r, r)
            elif abs(source - r) > 1:
                start, source = start if distance else t ^ 2, r
            pairs.append((start * rows + source, t * rows + r))
    return lax.ppermute(block, ("tm", "rows"), pairs)


def same(row, rows):
    return row


def across(row, rows):
    return (row + 1 if row % 2 else row - 1) % rows


def sibling(row, rows):
    return row ^ 1


def local(slc_stack, partner_count, look_sizes):
    cols = slc_stack.shape[-1]
    edge_16, edge_8 = ((16, cols), BF16), ((8, cols), BF16)
    next_1 = moved(slc_stack, 1, same)
    own, first_two, outer, outer_two = kernel(
        own_edges_kernel,
        "own_edges",
        [VMEM],
        [VMEM] * 4,
        [(slc_stack.shape, BF16), ((2,) + slc_stack.shape[1:], BF16), edge_16, edge_8],
        10**6,
        10**6,
    )(slc_stack)
    next_2 = moved(first_two, 2, same)
    outer_2 = moved(outer_two, 2, across)
    outer_1 = moved(outer, 1, across)
    (again,) = kernel(again_kernel, "again", [VMEM], [VMEM], [edge_16], 10**5, 10**5)(outer)
    own_outer = moved(again, 0, across)
    packed = look_sizes[:, 0] + 16 * look_sizes[:, 1] + 256 * partner_count
    main_weights, halo_weights, bands, factors = kernel(
        setup_kernel,
        "setup",
        [VMEM, pl.BlockSpec(memory_space=pl.ANY)],
        [VMEM] * 4,
        [
            ((4, FIELDS, FIELDS), BF16),
            ((4, FIELDS, 2 * WINDOW), BF16),
            ((4, 384, BLOCK), BF16),
            ((4, 16, 128), F32),
        ],
        10**6,
        2 * 10**6,
    )(packed[None], again)

    anywhere = pl.BlockSpec(memory_space=pl.ANY)

    def inner_edges(name, images, after):
        count = sum(image.shape[0] for image in images)
        return kernel(
            lambda after, *refs: inner_edges_kernel(*refs),
            name,
            [anywhere] + [VMEM] * len(images),
            [VMEM],
            [((4 * count, cols), BF16)],
            10**6,
            10**6,
        )(after, *images)[0]

    def row_sums(name, blocks, after):
        return kernel(
            lambda after, *refs: sums_kernel(*refs),
            name,
            [anywhere] + [VMEM] * (len(blocks) + 1),
            [VMEM],
            [((2, FIELDS, cols), F32)],
            2 * 10**9,
            3 * 10**6,
        )(after, *blocks, main_weights)[0]

    pair_shapes = [((2, MAXP, 2, ROWS, cols), BF16), ((2, MAXP, ROWS, cols), BF16)]
    scratch = [
        pltpu.VMEM((2, 2 * EDGE, cols), F32),
        pltpu.VMEM((2, FIELDS, cols + 2 * PAD), BF16),
    ]
    edges_1 = inner_edges("inner_1", (own, next_1), factors)
    inner_1 = moved(edges_1, 0, sibling)
    sums_1 = row_sums("sums_1", (own, next_1), edges_1)
    ifg, coh = kernel(
        functools.partial(windows_kernel, 0),
        "windows_1",
        [VMEM] * 7,
        [VMEM] * 2,
        pair_shapes,
        2 * 10**9,
        4 * 10**6,
        scratch,
    )(own_outer, outer_1, inner_1, halo_weights, bands, factors, sums_1)
    edges_2 = inner_edges("inner_2", (next_2,), coh)
    inner_2 = moved(edges_2, 0, sibling)
    sums_2 = row_sums("sums_2", (own, next_1, next_2), edges_2)
    return kernel(
        functools.partial(windows_kernel, 2),
        "windows_2",
        [VMEM] * 11,
        [pl.BlockSpec(memory_space=pl.ANY)] * 2,
        [((4, MAXP, 2, ROWS, cols), BF16), ((4, MAXP, ROWS, cols), BF16)],
        2 * 10**9,
        4 * 10**6,
        scratch + [pltpu.VMEM(*shape) for shape in pair_shapes] + [pltpu.SemaphoreType.DMA((6,))],
    )(
        own_outer, outer_1, inner_1, outer_2, inner_2, halo_weights, bands, factors,
        sums_2, ifg, coh,
    )


def solution(mesh):
    return jax.shard_map(
        local,
        mesh=mesh,
        in_specs=(P("tm", None, "rows", None), P("tm"), P("tm", None)),
        out_specs=(P("tm", None, None, "rows", None), P("tm", None, "rows", None)),
        check_vma=False,
    )
```

```python
import functools

import jax
import jax.numpy as jnp
from jax import lax
from jax.experimental import pallas as pl
from jax.experimental.pallas import tpu as pltpu
from jax.sharding import PartitionSpec as P

MAXP = 6
ROWS = 8
HALO = 2
NEAR = 10
EDGE = 24
FIELDS = 160
WINDOW = 96
BLOCK = 256
PAD = 128
UNROLL_SUMS = 8
UNROLL_HALO = 8
UNROLL_COLS = 8
epsilon = 1e-06
tiny = 1.1754944e-38
F32 = jnp.float32
BF16 = jnp.bfloat16


def iota(shape, dim):
    return lax.broadcasted_iota(jnp.int32, shape, dim)


def place():
    row = lax.axis_index("rows")
    return row, lax.rem(row, 2), lax.axis_size("rows")


def setup_kernel(packed, after, main_weights, halo_weights, bands, factors):
    row, core, row_total = place()
    numbers = [packed[:, a : a + 1] for a in range(4)]
    looks = [(n & 15, lax.shift_right_arithmetic(n, 4) & 15) for n in numbers]
    counts = [lax.shift_right_arithmetic(n, 8) for n in numbers]
    out_row = iota((8, 2 * FIELDS), 0)
    at = iota((8, 2 * FIELDS), 1)
    at = jnp.where(at >= FIELDS, at - FIELDS, at)
    main_field = lax.shift_right_arithmetic(at, 3)
    main_distance = jnp.abs((at & 7) - out_row)

    halo_row = iota((8, 2 * WINDOW), 0)
    at = iota((8, 2 * WINDOW), 1)
    at = jnp.where(at >= WINDOW, at - WINDOW, at)
    inner = at >= 48
    group = lax.shift_right_arithmetic(jnp.where(inner, at - 48, at), 4)
    near = lax.shift_right_arithmetic(at, 1) & 7
    slot_ok = (near >= 1) & (near <= 6)
    power_field = jnp.where(near <= 6, 12 + near, 99)
    halo_field = jnp.where(group == 2, power_field, jnp.where(slot_ok, 6 * group + near - 1, 99))
    above = jnp.where(inner, core, 1 - core) == 1
    position = (at & 1) + jnp.where(above, -HALO, ROWS)
    open_edge = jnp.where(core == 0, row > 0, row < row_total - 1)
    halo_field = jnp.where(inner | open_edge, halo_field, 99)
    halo_distance = jnp.abs(position - halo_row)

    for a in range(4):
        for weights, distance, field in (
            (main_weights, main_distance, main_field),
            (halo_weights, halo_distance, halo_field),
        ):
            hit = distance <= looks[a][0]
            for f in range(FIELDS // 16):
                pair = [jnp.where(hit & (field == 2 * f + i), 1.0, 0.0) for i in range(2)]
                weights[a, 16 * f : 16 * f + 16, :] = jnp.concatenate(pair, 0).astype(BF16)

    column = iota((384, BLOCK), 0)
    column = jnp.where(column < 320, column, column - 384)
    spread = jnp.abs(column - iota((384, BLOCK), 1))
    first_acq = lax.axis_index("tm") * 4
    acq_total = lax.axis_size("tm") * 4
    slot = iota((16, 128), 0)
    is_live = slot >= 8
    slot = slot & 7
    for a in range(4):
        bands[a] = jnp.where(spread <= looks[a][1], 1.0, 0.0).astype(BF16)
        live = (slot < counts[a]) & (first_acq + a + slot + 1 < acq_total)
        area = (2 * looks[a][0] + 1) * (2 * looks[a][1] + 1)
        area = jnp.broadcast_to(area, (16, 128)).astype(F32)
        values = jnp.where(live, jnp.where(is_live, 1.0, 1.0 / area), 0.0)
        for k in range(16):
            factors[a, k] = jnp.broadcast_to(values[k : k + 1], (8, 128))


def picked_edges(refs, wanted, cols):
    parts = []
    for ref in refs:
        for e in range(ref.shape[0]):
            parts += [ref[e, c, :, cols].astype(F32) for c in range(2)]
    data = jnp.concatenate(parts, 0).astype(BF16)
    pick = jnp.where(iota((wanted.shape[0], data.shape[0]), 1) == wanted, 1.0, 0.0)
    return jnp.dot(pick.astype(BF16), data, preferred_element_type=F32).astype(BF16)


def outer_rows(at, two, core):
    image = lax.shift_right_arithmetic(at, 1) & jnp.where(two, 1, 3)
    component = lax.shift_right_arithmetic(at, jnp.where(two, 2, 3))
    return (2 * image + component) * ROWS + (at & 1) + jnp.where(core == 1, ROWS - HALO, 0)


def blocks_of(ref):
    return [slice(n * BLOCK, (n + 1) * BLOCK) for n in range(ref.shape[-1] // BLOCK)]


def own_edges_kernel(images, own, first_two, outer, outer_two):
    core = place()[1]
    own[...] = images[...]
    first_two[...] = images[:2]
    to = iota((24, 64), 0)
    wanted = outer_rows(to & 15, to >= 16, core)
    for cols in blocks_of(own):
        edges = picked_edges((images,), wanted, cols)
        outer[:, cols] = edges[:16]
        outer_two[:, cols] = edges[16:]


def again_kernel(outer, outer_again):
    outer_again[...] = outer[...]


def inner_edges_kernel(*refs):
    core = place()[1]
    *images, inner = refs
    count = sum(ref.shape[0] for ref in images)
    to = iota((4 * count, 16 * count), 0)
    second = to >= 2 * count
    at = jnp.where(second, to - 2 * count, to)
    wanted = (at & -2) * ROWS + jnp.where(second, ROWS, 0) + (at & 1) + jnp.where(core == 0, ROWS - HALO, 0)
    for cols in blocks_of(inner):
        inner[:, cols] = picked_edges(images, wanted, cols)


def halves(terms):
    high = terms.astype(BF16)
    return high, (terms - high.astype(F32)).astype(BF16)


def sums_kernel(*refs):
    *blocks, main_weights, sums = refs
    near = [block.at[e] for block in blocks for e in range(block.shape[0])]
    first = len(near) - 2 - MAXP

    def body(n, carry):
        cols = pl.ds(pl.multiple_of(n * BLOCK, BLOCK), BLOCK)
        images = [(ref[0, :, cols].astype(F32), ref[1, :, cols].astype(F32)) for ref in near]
        powers = [re * re + im * im for re, im in images]
        for a in (first, first + 1):
            own_re, own_im = images[a]
            partners = images[a + 1 : a + 1 + MAXP]
            fields = [own_re * re + own_im * im for re, im in partners]
            fields += [own_im * re - own_re * im for re, im in partners]
            fields += powers[a : a + 1 + MAXP] + [jnp.zeros((ROWS, BLOCK), F32)]
            terms = jnp.concatenate(halves(jnp.concatenate(fields, 0)), 0)
            sums[a - first, :, cols] = jnp.dot(main_weights[a], terms, preferred_element_type=F32)
        return carry

    lax.fori_loop(0, sums.shape[-1] // BLOCK, body, 0, unroll=UNROLL_SUMS)


def repeated(tile, first):
    rows = iota(tile.shape, 0)
    kept = jnp.where((rows >= first) & (rows < first + 2), tile, 0.0)
    kept = kept + pltpu.roll(kept, 2, 0)
    return kept + pltpu.roll(kept, 4, 0)


def windows_kernel(first, *refs):
    own_outer, outer_1, inner_1, *refs = refs
    outer_2, inner_2, *refs = refs if first else (None, None, *refs)
    halo_weights, bands, factors, sums, *refs = refs
    if first:
        ifg_before, coh_before, ifg_out, coh_out, *refs = refs
        edge_rows, rounded, ifg, coh, sems = refs
        pieces = [(ifg_before, ifg_out, 0), (coh_before, coh_out, 0)]
        copies = []
        for k, (ref, out, at) in enumerate(pieces):
            copies.append(pltpu.make_async_copy(ref, out.at[at : at + 2], sems.at[k]))
            copies[-1].start()
    else:
        ifg, coh, edge_rows, rounded = refs
    cols_total = inner_1.shape[-1]
    blocks = cols_total // BLOCK
    rounded[:, :, :PAD] = jnp.zeros((2, FIELDS, PAD), BF16)
    rounded[:, :, PAD + cols_total :] = jnp.zeros((2, FIELDS, PAD), BF16)
    for c in range(2):
        at = EDGE * c
        edge_rows[0, at : at + 8, :] = own_outer[8 * c : 8 * c + 8].astype(F32)
        edge_rows[0, at + 8 : at + 16, :] = outer_1[8 * c : 8 * c + 8].astype(F32)
        edge_rows[1, at : at + 16, :] = inner_1[16 * c : 16 * c + 16].astype(F32)
        for h, ref in enumerate((outer_2, inner_2)):
            last = jnp.zeros((8, cols_total), F32)
            if first:
                last = ref[...].astype(F32)
                last = pltpu.roll(last, 4, 0) if c else last
                last = jnp.where(iota(last.shape, 0) < 4, last, 0.0)
            edge_rows[h, at + 16 : at + EDGE, :] = last

    def row_body(n, a):
        start = pl.multiple_of(n * BLOCK, BLOCK)
        cols = pl.ds(start, BLOCK)
        fields = []
        for h in range(2):
            mine = []
            for c in range(2):
                at = c * EDGE + 2 * a
                tile = edge_rows[h, at // 8 * 8 : at // 8 * 8 + 8, cols]
                mine.append(repeated(tile, at % 8))
            own_re, own_im = mine
            images = []
            for half in range(2):
                at = 2 * a + 8 * half
                images.append((edge_rows[h, at : at + 8, cols], edge_rows[h, at + EDGE : at + EDGE + 8, cols]))
            fields += [own_re * re + own_im * im for re, im in images]
            fields += [own_im * re - own_re * im for re, im in images]
            fields += [re * re + im * im for re, im in images]
        terms = jnp.concatenate(halves(jnp.concatenate(fields, 0)), 0)
        total = sums[a - first, :, cols] + jnp.dot(halo_weights[a], terms, preferred_element_type=F32)
        rounded[a % 2, :, pl.ds(pl.multiple_of(start + PAD, 128), BLOCK)] = total.astype(BF16)

    def col_body(n, a):
        start = pl.multiple_of(n * BLOCK, BLOCK)
        cols = pl.ds(start, BLOCK)
        inside = rounded[a % 2, :, pl.ds(pl.multiple_of(start + PAD, 128), BLOCK)]
        left = rounded[a % 2, :, pl.ds(start, PAD)]
        right = rounded[a % 2, :, pl.ds(pl.multiple_of(start + PAD + BLOCK, 128), PAD)]
        sides = jnp.where(iota((FIELDS, PAD), 1) < 64, right, left)
        boxed = jnp.dot(jnp.concatenate([inside, sides], 1), bands[a], preferred_element_type=F32)
        own_power = boxed[96:104]
        for j in range(MAXP):
            re = boxed[8 * j : 8 * j + 8]
            im = boxed[48 + 8 * j : 56 + 8 * j]
            power = boxed[104 + 8 * j : 112 + 8 * j]
            scale = jnp.concatenate([factors[a, j]] * 2, 1)
            live = jnp.concatenate([factors[a, 8 + j]] * 2, 1)
            ifg[a - first, j, 0, :, cols] = (re * scale).astype(BF16)
            ifg[a - first, j, 1, :, cols] = (im * scale).astype(BF16)
            square = re * re + im * im
            magnitude = square * lax.rsqrt(jnp.maximum(square, tiny))
            coherence = magnitude * lax.rsqrt(own_power * power + epsilon) * live
            coh[a - first, j, :, cols] = coherence.astype(BF16)

    def loop(body, a, unroll):
        lax.fori_loop(0, blocks, lambda n, carry: (body(n, a), carry)[1], 0, unroll=unroll)

    def both_body(n, a):
        col_body(n, a)
        row_body(n, a + 1)

    loop(row_body, first, UNROLL_HALO)
    loop(both_body, first, UNROLL_COLS)
    def send(a):
        if first:
            for k, (scratch, out) in enumerate(((ifg, ifg_out), (coh, coh_out))):
                copy = pltpu.make_async_copy(scratch.at[a - first], out.at[a], sems.at[2 * (a - first + 1) + k])
                copy.start()
                copies.append(copy)

    send(first)
    loop(col_body, first + 1, UNROLL_COLS)
    send(first + 1)
    if first:
        for copy in copies:
            copy.wait()


VMEM = pl.BlockSpec(memory_space=pltpu.VMEM)
SMEM = pl.BlockSpec(memory_space=pltpu.SMEM)


def kernel(body, name, in_specs, out_specs, out_shape, flops, moved, scratch=(), limit=40):
    return pl.pallas_call(
        body,
        in_specs=in_specs,
        out_specs=out_specs,
        out_shape=[jax.ShapeDtypeStruct(*s) for s in out_shape],
        scratch_shapes=scratch,
        compiler_params=pltpu.CompilerParams(vmem_limit_bytes=limit * 2**20),
        cost_estimate=pl.CostEstimate(flops=flops, bytes_accessed=moved, transcendentals=0),
        name=name,
    )


def moved(block, distance, partner):
    count, rows = lax.axis_size("tm"), lax.axis_size("rows")
    half = rows // 2
    pairs = []
    for t in range(count):
        for r in range(rows):
            start, source = (t + distance) % count, partner(r, rows)
            if t + distance >= count:
                late = {half - 1: rows - 1, half: rows - 2, rows - 1: half - 1, rows - 2: half}
                source = (r + half) % rows if distance == 1 else r
                if distance == 2 and partner is same:
                    source = late.get(r, r)
            elif abs(source - r) > 1:
                start, source = start if distance else t ^ 2, r
            pairs.append((start * rows + source, t * rows + r))
    return lax.ppermute(block, ("tm", "rows"), pairs)


def same(row, rows):
    return row


def across(row, rows):
    return (row + 1 if row % 2 else row - 1) % rows


def sibling(row, rows):
    return row ^ 1


def local(slc_stack, partner_count, look_sizes):
    cols = slc_stack.shape[-1]
    edge_16, edge_8 = ((16, cols), BF16), ((8, cols), BF16)
    next_1 = moved(slc_stack, 1, same)
    own, first_two, outer, outer_two = kernel(
        own_edges_kernel,
        "own_edges",
        [VMEM],
        [VMEM] * 4,
        [(slc_stack.shape, BF16), ((2,) + slc_stack.shape[1:], BF16), edge_16, edge_8],
        10**6,
        10**6,
    )(slc_stack)
    next_2 = moved(first_two, 2, same)
    outer_2 = moved(outer_two, 2, across)
    outer_1 = moved(outer, 1, across)
    (again,) = kernel(again_kernel, "again", [VMEM], [VMEM], [edge_16], 10**5, 10**5)(outer)
    own_outer = moved(again, 0, across)
    packed = look_sizes[:, 0] + 16 * look_sizes[:, 1] + 256 * partner_count
    main_weights, halo_weights, bands, factors = kernel(
        setup_kernel,
        "setup",
        [VMEM, pl.BlockSpec(memory_space=pl.ANY)],
        [VMEM] * 4,
        [
            ((4, FIELDS, 2 * FIELDS), BF16),
            ((4, FIELDS, 2 * WINDOW), BF16),
            ((4, 384, BLOCK), BF16),
            ((4, 16, 8, 128), F32),
        ],
        10**6,
        2 * 10**6,
    )(packed[None], again)

    anywhere = pl.BlockSpec(memory_space=pl.ANY)

    def inner_edges(name, images, after):
        count = sum(image.shape[0] for image in images)
        return kernel(
            lambda after, *refs: inner_edges_kernel(*refs),
            name,
            [anywhere] + [VMEM] * len(images),
            [VMEM],
            [((4 * count, cols), BF16)],
            10**6,
            10**6,
        )(after, *images)[0]

    def row_sums(name, blocks, after):
        return kernel(
            lambda after, *refs: sums_kernel(*refs),
            name,
            [anywhere] + [VMEM] * (len(blocks) + 1),
            [VMEM],
            [((2, FIELDS, cols), F32)],
            2 * 10**9,
            3 * 10**6,
        )(after, *blocks, main_weights)[0]

    pair_shapes = [((2, MAXP, 2, ROWS, cols), BF16), ((2, MAXP, ROWS, cols), BF16)]
    scratch = [
        pltpu.VMEM((2, 2 * EDGE, cols), F32),
        pltpu.VMEM((2, FIELDS, cols + 2 * PAD), BF16),
    ]
    edges_1 = inner_edges("inner_1", (own, next_1), factors)
    inner_1 = moved(edges_1, 0, sibling)
    sums_1 = row_sums("sums_1", (own, next_1), edges_1)
    ifg, coh = kernel(
        functools.partial(windows_kernel, 0),
        "windows_1",
        [VMEM] * 7,
        [VMEM] * 2,
        pair_shapes,
        2 * 10**9,
        4 * 10**6,
        scratch,
    )(own_outer, outer_1, inner_1, halo_weights, bands, factors, sums_1)
    edges_2 = inner_edges("inner_2", (next_2,), coh)
    inner_2 = moved(edges_2, 0, sibling)
    sums_2 = row_sums("sums_2", (own, next_1, next_2), edges_2)
    return kernel(
        functools.partial(windows_kernel, 2),
        "windows_2",
        [VMEM] * 11,
        [pl.BlockSpec(memory_space=pl.ANY)] * 2,
        [((4, MAXP, 2, ROWS, cols), BF16), ((4, MAXP, ROWS, cols), BF16)],
        2 * 10**9,
        4 * 10**6,
        scratch + [pltpu.VMEM(*shape) for shape in pair_shapes] + [pltpu.SemaphoreType.DMA((6,))],
    )(
        own_outer, outer_1, inner_1, outer_2, inner_2, halo_weights, bands, factors,
        sums_2, ifg, coh,
    )


def solution(mesh):
    return jax.shard_map(
        local,
        mesh=mesh,
        in_specs=(P("tm", None, "rows", None), P("tm"), P("tm", None)),
        out_specs=(P("tm", None, None, "rows", None), P("tm", None, "rows", None)),
        check_vma=False,
    )
```

```python
import functools

import jax
import jax.numpy as jnp
from jax import lax
from jax.experimental import pallas as pl
from jax.experimental.pallas import tpu as pltpu
from jax.sharding import PartitionSpec as P

MAXP = 6
ROWS = 8
HALO = 2
NEAR = 10
EDGE = 24
FIELDS = 160
WINDOW = 96
BLOCK = 256
PAD = 128
UNROLL_SUMS = 8
UNROLL_HALO = 8
UNROLL_COLS = 8
epsilon = 1e-06
tiny = 1.1754944e-38
F32 = jnp.float32
BF16 = jnp.bfloat16


def iota(shape, dim):
    return lax.broadcasted_iota(jnp.int32, shape, dim)


def place():
    row = lax.axis_index("rows")
    return row, lax.rem(row, 2), lax.axis_size("rows")


def setup_kernel(packed, after, main_weights, halo_weights, bands, factors):
    row, core, row_total = place()
    numbers = [packed[:, a : a + 1] for a in range(4)]
    looks = [(n & 15, lax.shift_right_arithmetic(n, 4) & 15) for n in numbers]
    counts = [lax.shift_right_arithmetic(n, 8) for n in numbers]
    out_row = iota((8, 2 * FIELDS), 0)
    at = iota((8, 2 * FIELDS), 1)
    at = jnp.where(at >= FIELDS, at - FIELDS, at)
    main_field = lax.shift_right_arithmetic(at, 3)
    main_distance = jnp.abs((at & 7) - out_row)

    halo_row = iota((8, 2 * WINDOW), 0)
    at = iota((8, 2 * WINDOW), 1)
    at = jnp.where(at >= WINDOW, at - WINDOW, at)
    inner = at >= 48
    group = lax.shift_right_arithmetic(jnp.where(inner, at - 48, at), 4)
    near = lax.shift_right_arithmetic(at, 1) & 7
    slot_ok = (near >= 1) & (near <= 6)
    power_field = jnp.where(near <= 6, 12 + near, 99)
    halo_field = jnp.where(group == 2, power_field, jnp.where(slot_ok, 6 * group + near - 1, 99))
    above = jnp.where(inner, core, 1 - core) == 1
    position = (at & 1) + jnp.where(above, -HALO, ROWS)
    open_edge = jnp.where(core == 0, row > 0, row < row_total - 1)
    halo_field = jnp.where(inner | open_edge, halo_field, 99)
    halo_distance = jnp.abs(position - halo_row)

    for a in range(4):
        for weights, distance, field in (
            (main_weights, main_distance, main_field),
            (halo_weights, halo_distance, halo_field),
        ):
            hit = distance <= looks[a][0]
            for f in range(FIELDS // 16):
                pair = [jnp.where(hit & (field == 2 * f + i), 1.0, 0.0) for i in range(2)]
                weights[a, 16 * f : 16 * f + 16, :] = jnp.concatenate(pair, 0).astype(BF16)

    column = iota((384, BLOCK), 0)
    column = jnp.where(column < 320, column, column - 384)
    spread = jnp.abs(column - iota((384, BLOCK), 1))
    first_acq = lax.axis_index("tm") * 4
    acq_total = lax.axis_size("tm") * 4
    slot = iota((16, 128), 0)
    is_live = slot >= 8
    slot = slot & 7
    for a in range(4):
        bands[a] = jnp.where(spread <= looks[a][1], 1.0, 0.0).astype(BF16)
        live = (slot < counts[a]) & (first_acq + a + slot + 1 < acq_total)
        area = (2 * looks[a][0] + 1) * (2 * looks[a][1] + 1)
        area = jnp.broadcast_to(area, (16, 128)).astype(F32)
        values = jnp.where(live, jnp.where(is_live, 1.0, 1.0 / area), 0.0)
        for k in range(16):
            factors[a, k] = jnp.broadcast_to(values[k : k + 1], (8, 128))


def picked_edges(refs, wanted, cols):
    parts = []
    for ref in refs:
        for e in range(ref.shape[0]):
            parts += [ref[e, c, :, cols].astype(F32) for c in range(2)]
    data = jnp.concatenate(parts, 0).astype(BF16)
    pick = jnp.where(iota((wanted.shape[0], data.shape[0]), 1) == wanted, 1.0, 0.0)
    return jnp.dot(pick.astype(BF16), data, preferred_element_type=F32).astype(BF16)


def outer_rows(at, two, core):
    image = lax.shift_right_arithmetic(at, 1) & jnp.where(two, 1, 3)
    component = lax.shift_right_arithmetic(at, jnp.where(two, 2, 3))
    return (2 * image + component) * ROWS + (at & 1) + jnp.where(core == 1, ROWS - HALO, 0)


def blocks_of(ref):
    return [slice(n * BLOCK, (n + 1) * BLOCK) for n in range(ref.shape[-1] // BLOCK)]


def own_edges_kernel(images, own, first_two, outer, outer_two):
    core = place()[1]
    own[...] = images[...]
    first_two[...] = images[:2]
    to = iota((24, 64), 0)
    wanted = outer_rows(to & 15, to >= 16, core)
    for cols in blocks_of(own):
        edges = picked_edges((images,), wanted, cols)
        outer[:, cols] = edges[:16]
        outer_two[:, cols] = edges[16:]


def again_kernel(outer, outer_again):
    outer_again[...] = outer[...]


def inner_edges_kernel(*refs):
    core = place()[1]
    *images, inner = refs
    count = sum(ref.shape[0] for ref in images)
    to = iota((4 * count, 16 * count), 0)
    second = to >= 2 * count
    at = jnp.where(second, to - 2 * count, to)
    wanted = (at & -2) * ROWS + jnp.where(second, ROWS, 0) + (at & 1) + jnp.where(core == 0, ROWS - HALO, 0)
    for cols in blocks_of(inner):
        inner[:, cols] = picked_edges(images, wanted, cols)


def halves(terms):
    high = terms.astype(BF16)
    return high, (terms - high.astype(F32)).astype(BF16)


def sums_kernel(*refs):
    *blocks, main_weights, sums = refs
    near = [block.at[e] for block in blocks for e in range(block.shape[0])]
    first = len(near) - 2 - MAXP

    def body(n, carry):
        cols = pl.ds(pl.multiple_of(n * BLOCK, BLOCK), BLOCK)
        images = [(ref[0, :, cols].astype(F32), ref[1, :, cols].astype(F32)) for ref in near]
        powers = [re * re + im * im for re, im in images]
        for a in (first, first + 1):
            own_re, own_im = images[a]
            partners = images[a + 1 : a + 1 + MAXP]
            fields = [own_re * re + own_im * im for re, im in partners]
            fields += [own_im * re - own_re * im for re, im in partners]
            fields += powers[a : a + 1 + MAXP] + [jnp.zeros((ROWS, BLOCK), F32)]
            terms = jnp.concatenate(halves(jnp.concatenate(fields, 0)), 0)
            sums[a - first, :, cols] = jnp.dot(main_weights[a], terms, preferred_element_type=F32)
        return carry

    lax.fori_loop(0, sums.shape[-1] // BLOCK, body, 0, unroll=UNROLL_SUMS)


def repeated(tile, first):
    rows = iota(tile.shape, 0)
    kept = jnp.where((rows >= first) & (rows < first + 2), tile, 0.0)
    kept = kept + pltpu.roll(kept, 2, 0)
    return kept + pltpu.roll(kept, 4, 0)


def windows_kernel(first, *refs):
    own_outer, outer_1, inner_1, *refs = refs
    outer_2, inner_2, *refs = refs if first else (None, None, *refs)
    halo_weights, bands, factors, sums, *refs = refs
    if first:
        ifg_before, coh_before, ifg_out, coh_out, *refs = refs
        edge_rows, rounded, ifg, coh, sems = refs
        pieces = [(ifg_before, ifg_out, 0), (coh_before, coh_out, 0)]
        copies = []
        for k, (ref, out, at) in enumerate(pieces):
            copies.append(pltpu.make_async_copy(ref, out.at[at : at + 2], sems.at[k]))
            copies[-1].start()
    else:
        ifg, coh, edge_rows, rounded = refs
    cols_total = inner_1.shape[-1]
    blocks = cols_total // BLOCK
    rounded[:, :, :PAD] = jnp.zeros((2, FIELDS, PAD), BF16)
    rounded[:, :, PAD + cols_total :] = jnp.zeros((2, FIELDS, PAD), BF16)
    for c in range(2):
        at = EDGE * c
        edge_rows[0, at : at + 8, :] = own_outer[...].astype(F32)[8 * c : 8 * c + 8]
        edge_rows[0, at + 8 : at + 16, :] = outer_1[...].astype(F32)[8 * c : 8 * c + 8]
        edge_rows[1, at : at + 16, :] = inner_1[16 * c : 16 * c + 16].astype(F32)
        for h, ref in enumerate((outer_2, inner_2)):
            last = jnp.zeros((8, cols_total), F32)
            if first:
                last = ref[...].astype(F32)
                last = pltpu.roll(last, 4, 0) if c else last
                last = jnp.where(iota(last.shape, 0) < 4, last, 0.0)
            edge_rows[h, at + 16 : at + EDGE, :] = last

    def row_body(n, a):
        start = pl.multiple_of(n * BLOCK, BLOCK)
        cols = pl.ds(start, BLOCK)
        fields = []
        for h in range(2):
            mine = []
            for c in range(2):
                at = c * EDGE + 2 * a
                tile = edge_rows[h, at // 8 * 8 : at // 8 * 8 + 8, cols]
                mine.append(repeated(tile, at % 8))
            own_re, own_im = mine
            images = []
            for half in range(2):
                at = 2 * a + 8 * half
                images.append((edge_rows[h, at : at + 8, cols], edge_rows[h, at + EDGE : at + EDGE + 8, cols]))
            fields += [own_re * re + own_im * im for re, im in images]
            fields += [own_im * re - own_re * im for re, im in images]
            fields += [re * re + im * im for re, im in images]
        terms = jnp.concatenate(halves(jnp.concatenate(fields, 0)), 0)
        total = sums[a - first, :, cols] + jnp.dot(halo_weights[a], terms, preferred_element_type=F32)
        rounded[a % 2, :, pl.ds(pl.multiple_of(start + PAD, 128), BLOCK)] = total.astype(BF16)

    def col_body(n, a):
        start = pl.multiple_of(n * BLOCK, BLOCK)
        cols = pl.ds(start, BLOCK)
        inside = rounded[a % 2, :, pl.ds(pl.multiple_of(start + PAD, 128), BLOCK)]
        left = rounded[a % 2, :, pl.ds(start, PAD)]
        right = rounded[a % 2, :, pl.ds(pl.multiple_of(start + PAD + BLOCK, 128), PAD)]
        sides = jnp.where(iota((FIELDS, PAD), 1) < 64, right, left)
        boxed = jnp.dot(jnp.concatenate([inside, sides], 1), bands[a], preferred_element_type=F32)
        own_power = boxed[96:104]
        for j in range(MAXP):
            re = boxed[8 * j : 8 * j + 8]
            im = boxed[48 + 8 * j : 56 + 8 * j]
            power = boxed[104 + 8 * j : 112 + 8 * j]
            scale = jnp.concatenate([factors[a, j]] * 2, 1)
            live = jnp.concatenate([factors[a, 8 + j]] * 2, 1)
            ifg[a - first, j, 0, :, cols] = (re * scale).astype(BF16)
            ifg[a - first, j, 1, :, cols] = (im * scale).astype(BF16)
            square = re * re + im * im
            magnitude = square * lax.rsqrt(jnp.maximum(square, tiny))
            coherence = magnitude * lax.rsqrt(own_power * power + epsilon) * live
            coh[a - first, j, :, cols] = coherence.astype(BF16)

    def loop(body, a, unroll):
        lax.fori_loop(0, blocks, lambda n, carry: (body(n, a), carry)[1], 0, unroll=unroll)

    def both_body(n, a):
        col_body(n, a)
        row_body(n, a + 1)

    loop(row_body, first, UNROLL_HALO)
    loop(both_body, first, UNROLL_COLS)
    def send(a):
        if first:
            for k, (scratch, out) in enumerate(((ifg, ifg_out), (coh, coh_out))):
                copy = pltpu.make_async_copy(scratch.at[a - first], out.at[a], sems.at[2 * (a - first + 1) + k])
                copy.start()
                copies.append(copy)

    send(first)
    loop(col_body, first + 1, UNROLL_COLS)
    send(first + 1)
    if first:
        for copy in copies:
            copy.wait()


VMEM = pl.BlockSpec(memory_space=pltpu.VMEM)
SMEM = pl.BlockSpec(memory_space=pltpu.SMEM)


def kernel(body, name, in_specs, out_specs, out_shape, flops, moved, scratch=(), limit=40):
    return pl.pallas_call(
        body,
        in_specs=in_specs,
        out_specs=out_specs,
        out_shape=[jax.ShapeDtypeStruct(*s) for s in out_shape],
        scratch_shapes=scratch,
        compiler_params=pltpu.CompilerParams(vmem_limit_bytes=limit * 2**20),
        cost_estimate=pl.CostEstimate(flops=flops, bytes_accessed=moved, transcendentals=0),
        name=name,
    )


def moved(block, distance, partner):
    count, rows = lax.axis_size("tm"), lax.axis_size("rows")
    half = rows // 2
    pairs = []
    for t in range(count):
        for r in range(rows):
            start, source = (t + distance) % count, partner(r, rows)
            if t + distance >= count:
                late = {half - 1: rows - 1, half: rows - 2, rows - 1: half - 1, rows - 2: half}
                source = (r + half) % rows if distance == 1 else r
                if distance == 2 and partner is same:
                    source = late.get(r, r)
            elif abs(source - r) > 1:
                start, source = start if distance else t ^ 2, r
            pairs.append((start * rows + source, t * rows + r))
    return lax.ppermute(block, ("tm", "rows"), pairs)


def same(row, rows):
    return row


def across(row, rows):
    return (row + 1 if row % 2 else row - 1) % rows


def sibling(row, rows):
    return row ^ 1


def local(slc_stack, partner_count, look_sizes):
    cols = slc_stack.shape[-1]
    edge_16, edge_8 = ((16, cols), BF16), ((8, cols), BF16)
    next_1 = moved(slc_stack, 1, same)
    own, first_two, outer, outer_two = kernel(
        own_edges_kernel,
        "own_edges",
        [VMEM],
        [VMEM] * 4,
        [(slc_stack.shape, BF16), ((2,) + slc_stack.shape[1:], BF16), edge_16, edge_8],
        10**6,
        10**6,
    )(slc_stack)
    next_2 = moved(first_two, 2, same)
    outer_2 = moved(outer_two, 2, across)
    outer_1 = moved(outer, 1, across)
    (again,) = kernel(again_kernel, "again", [VMEM], [VMEM], [edge_16], 10**5, 10**5)(outer)
    own_outer = moved(again, 0, across)
    packed = look_sizes[:, 0] + 16 * look_sizes[:, 1] + 256 * partner_count
    main_weights, halo_weights, bands, factors = kernel(
        setup_kernel,
        "setup",
        [VMEM, pl.BlockSpec(memory_space=pl.ANY)],
        [VMEM] * 4,
        [
            ((4, FIELDS, 2 * FIELDS), BF16),
            ((4, FIELDS, 2 * WINDOW), BF16),
            ((4, 384, BLOCK), BF16),
            ((4, 16, 8, 128), F32),
        ],
        10**6,
        2 * 10**6,
    )(packed[None], again)

    anywhere = pl.BlockSpec(memory_space=pl.ANY)

    def inner_edges(name, images, after):
        count = sum(image.shape[0] for image in images)
        return kernel(
            lambda after, *refs: inner_edges_kernel(*refs),
            name,
            [anywhere] + [VMEM] * len(images),
            [VMEM],
            [((4 * count, cols), BF16)],
            10**6,
            10**6,
        )(after, *images)[0]

    def row_sums(name, blocks, after):
        return kernel(
            lambda after, *refs: sums_kernel(*refs),
            name,
            [anywhere] + [VMEM] * (len(blocks) + 1),
            [VMEM],
            [((2, FIELDS, cols), F32)],
            2 * 10**9,
            3 * 10**6,
        )(after, *blocks, main_weights)[0]

    pair_shapes = [((2, MAXP, 2, ROWS, cols), BF16), ((2, MAXP, ROWS, cols), BF16)]
    scratch = [
        pltpu.VMEM((2, 2 * EDGE, cols), F32),
        pltpu.VMEM((2, FIELDS, cols + 2 * PAD), BF16),
    ]
    edges_1 = inner_edges("inner_1", (own, next_1), factors)
    inner_1 = moved(edges_1, 0, sibling)
    sums_1 = row_sums("sums_1", (own, next_1), edges_1)
    ifg, coh = kernel(
        functools.partial(windows_kernel, 0),
        "windows_1",
        [VMEM] * 7,
        [VMEM] * 2,
        pair_shapes,
        2 * 10**9,
        4 * 10**6,
        scratch,
    )(own_outer, outer_1, inner_1, halo_weights, bands, factors, sums_1)
    edges_2 = inner_edges("inner_2", (next_2,), coh)
    inner_2 = moved(edges_2, 0, sibling)
    sums_2 = row_sums("sums_2", (own, next_1, next_2), edges_2)
    return kernel(
        functools.partial(windows_kernel, 2),
        "windows_2",
        [VMEM] * 11,
        [pl.BlockSpec(memory_space=pl.ANY)] * 2,
        [((4, MAXP, 2, ROWS, cols), BF16), ((4, MAXP, ROWS, cols), BF16)],
        2 * 10**9,
        4 * 10**6,
        scratch + [pltpu.VMEM(*shape) for shape in pair_shapes] + [pltpu.SemaphoreType.DMA((6,))],
    )(
        own_outer, outer_1, inner_1, outer_2, inner_2, halo_weights, bands, factors,
        sums_2, ifg, coh,
    )


def solution(mesh):
    return jax.shard_map(
        local,
        mesh=mesh,
        in_specs=(P("tm", None, "rows", None), P("tm"), P("tm", None)),
        out_specs=(P("tm", None, None, "rows", None), P("tm", None, "rows", None)),
        check_vma=False,
    )
```
